256 devices in a mesh: seq: 32 (over x, z), fsdp: 8 (over y, core).
Axes of the slice: x: 4, y: 4, z: 8, core: 2. Of those that a mesh axis runs over, the one named last changes fastest.
Arguments:
- frames: bfloat16 [8, 4096, 1536], P('fsdp', 'seq'), may hold values from -6 to 6
- lengths: int32 [8, 4], P('fsdp'), may hold values from 1 to 2048, 4096 in all within a row
- offsets: int32 [8, 33], P('fsdp'), may hold values from 0 to 4096, as said below
- w_in: bfloat16 [1536, 3072], P('fsdp'), may hold values from -0.15625 to 0.15625
- kernel: float32 [31, 1536], replicated, may hold values from -1 to 1
- cotangent: bfloat16 [8, 8192, 1536], P('fsdp', 'seq'), may hold values from -6 to 6
Outputs:
- owner_output: bfloat16 [8, 8192, 1536], P('fsdp', 'seq')
- frame_grad: bfloat16 [8, 4096, 1536], P('fsdp', 'seq')
- w_grad: float32 [1536, 3072], P(('seq', 'fsdp'))
The draws below stay inside these ranges and needn't reach their ends.
Inputs may be any that keep to these rules, and one draw needn't show every extreme that they name: Row g: device i of seq owns the frames offsets[g, i] to offsets[g, i + 1] - 1; offsets[g, 0] = 0 and offsets[g, 32] = 4096; each device owns 128 // 4 to 256 frames, beginning within 64 of i * 128; in every group one device owns exactly 256. `lengths`: each row sums to 4096; its largest entry is exactly 2048.
All inputs are finite; a program needn't handle non-finite values.
Results may differ from the reference program's by a relative error of at most 0.025.
Values may be sent and summed in bfloat16 or wider, within the bound.
No kernel may reach another device: no remote copies, remote signals or barrier semaphores. Data moves between devices by JAX's collectives and lax.ppermute only.
A program may use at most 128 MiB of HBM per device.

```python
import math
import jax
import jax.numpy as jnp
import numpy as np
from jax import lax

D = 1536
KW = 31
UTTS = 4
TOK_DEV = 128
FRAMES = 4096
SLOTS = 8192
GROUPS = 8


def draw_offsets(key, part):
    quarter = TOK_DEV // 4
    half_block = TOK_DEV // 2
    seq_count = FRAMES // TOK_DEV
    first_key, second_key = jax.random.split(jax.random.fold_in(key, 11))
    shifts = jax.random.randint(first_key, (GROUPS, seq_count + 1), -quarter, quarter + 1)
    picked = jax.random.randint(second_key, (GROUPS, 1), 1, seq_count - 1)
    column = jnp.arange(seq_count + 1, dtype=jnp.int32)[None, :]
    shifts = jnp.where(column == picked, -half_block, shifts)
    shifts = jnp.where(column == picked + 1, half_block, shifts)
    shifts = jnp.where((column == 0) | (column == seq_count), 0, shifts)
    return (column * TOK_DEV + shifts).astype(jnp.int32)


def strengthened(array, own_key, source, target, parts, factor):
    owner, partner = [(jnp.arange(array.shape[position]) // (array.shape[position] // parts)).reshape([-1 if axis == position else 1 for axis in range(array.ndim)]) for position in (source, target)]
    chosen = jax.random.permutation(own_key, parts)[partner]
    strong = (owner == chosen) | (owner == (partner + parts // 2) % parts)
    return jnp.where(strong, factor * array, array)


def block_levels(own_key, shape, cuts, least, largest):
    factor_of = 1.0
    for axis_at, shards_of in cuts:
        draws = jax.random.uniform(jax.random.fold_in(jax.random.fold_in(own_key, 6), axis_at), (shards_of,), jnp.float32, least / len(cuts), largest / len(cuts))
        factor_of = factor_of * jnp.repeat(jnp.exp(draws), shape[axis_at] // shards_of).reshape((-1,) + (1,) * (len(shape) - 1 - axis_at))
    return factor_of


def length_profile(amount, total, reach, slope):
    weights = [(1 << 20) // math.isqrt(grade ** slope) + 1 for grade in range(2, amount + 1)]
    surplus, given = total - reach - (amount - 1), [1] * (amount - 1)
    while surplus > 0:
        movable = [i for i in range(amount - 1) if given[i] < reach]
        pool, budget = sum([weights[i] for i in movable]), surplus
        for i in movable:
            addition = min(reach - given[i], max(1, budget * weights[i] // pool), surplus)
            given[i] = given[i] + addition
            surplus = surplus - addition
    return np.array([reach] + given)


def uneven(key, count, total, reach, lean):
    if count == 2:
        one = jax.random.randint(key, (), max(1, total - reach), min(reach, total - 1) + 1)
        return jnp.stack([one, total - one])
    sizes = jnp.asarray(length_profile(count, total, reach, lean), jnp.int32)
    twos = (count - 1) // 2
    donor, taker = sizes[1:1 + 2 * twos:2], sizes[2:2 + 2 * twos:2]
    room = jnp.minimum(donor - 1, reach - taker)
    passed = jax.random.randint(jax.random.fold_in(key, 1), (twos,), 0, 1 << 20) % (room + 1)
    sizes = sizes.at[1:1 + 2 * twos:2].set(donor - passed).at[2:2 + 2 * twos:2].set(taker + passed)
    return sizes[jax.random.permutation(jax.random.fold_in(key, 2), count)]


def gaussian(own_key, dims, scale, bound, pieces=(), kind=jnp.bfloat16):
    values = scale * jax.random.normal(own_key, dims, jnp.float32)
    if pieces:
        values = values * block_levels(own_key, dims, pieces, -0.22, 0.18)
    return jnp.clip(values, -bound, bound).astype(kind)


def bell_draw_with(stream_key, dims, spread, limit, pieces, heavy, kind=jnp.bfloat16):
    values = spread * jax.random.normal(stream_key, dims, jnp.float32)
    if pieces:
        values = values * block_levels(stream_key, dims, pieces, -0.22, 0.18)
    return jnp.clip(strengthened(values, jax.random.fold_in(stream_key, 3), *heavy), -limit, limit).astype(kind)


def setup_inputs(seed: int = 0) -> dict:
    key_list = jax.random.split(jax.random.key(seed), 7)
    return {
        "frames": gaussian(key_list[0], (GROUPS, FRAMES, D), 1.0, 6.0, ((0, 8), (1, 32))),
        "lengths": jax.vmap(lambda own: uneven(own, UTTS, FRAMES, FRAMES // 2, 1))(jax.random.split(key_list[1], GROUPS)).reshape((GROUPS, UTTS)).astype(jnp.int32),
        "offsets": draw_offsets(jax.random.fold_in(key_list[6], 71), 0),
        "w_in": gaussian(key_list[3], (D, 2 * D), D ** -0.5, 0.15625, ((0, 8),)),
        "kernel": gaussian(key_list[4], (KW, D), KW ** -0.5, 1.0, (), jnp.float32),
        "cotangent": bell_draw_with(key_list[5], (GROUPS, SLOTS, D), 1.0, 6.0, ((0, 8), (1, 32)), (1, 2, 32, 2.75)),
    }


epsilon = 1e-05

def normalize_rows(values):
    values = values.astype(jnp.float32)
    center = lax.optimization_barrier(jnp.mean(values, axis=-1, keepdims=True))
    shifted = values - center
    scale_inv = lax.rsqrt(lax.optimization_barrier(jnp.mean(shifted * shifted, axis=-1, keepdims=True)) + epsilon)
    return (shifted * scale_inv, scale_inv)

def norm_backward(upstream, normed, scale_inv):
    first_mean = lax.optimization_barrier(jnp.mean(upstream, axis=-1, keepdims=True))
    second_mean = lax.optimization_barrier(jnp.mean(upstream * normed, axis=-1, keepdims=True))
    return scale_inv * (upstream - first_mean - normed * second_mean)

def utterance_of(positions, lens_row, frame_total):
    bounds = jnp.cumsum(lens_row)[:-1]
    labels = lax.optimization_barrier(jnp.sum((positions[:, None] >= bounds[None, :]).astype(jnp.int32), axis=1))
    inside = (positions >= 0) & (positions < frame_total)
    return jnp.where(inside, labels, -1).astype(jnp.int32)

def depthwise(window, kernel, labels, row_count):
    tap_count = kernel.shape[0]
    half_width = tap_count // 2
    centre = labels[half_width:half_width + row_count]
    result = jnp.zeros((row_count, kernel.shape[1]), jnp.float32)
    for tap_index in range(tap_count):
        same_utt = (labels[tap_index:tap_index + row_count] == centre).astype(jnp.float32)
        result = result + kernel[tap_index] * window[tap_index:tap_index + row_count].astype(jnp.float32) * same_utt[:, None]
    return result

def depthwise_back(window, kernel, labels, row_count):
    tap_count = kernel.shape[0]
    half_width = tap_count // 2
    centre = labels[half_width:half_width + row_count]
    result = jnp.zeros((row_count, kernel.shape[1]), jnp.float32)
    for tap_index in range(tap_count):
        tap_row = 2 * half_width - tap_index
        same_utt = (labels[tap_row:tap_row + row_count] == centre).astype(jnp.float32)
        result = result + kernel[tap_index] * window[tap_row:tap_row + row_count] * same_utt[:, None]
    return result

def reference(frames, lengths, offsets, w_in, kernel, cotangent):
    group_count, frame_total, model_width = frames.shape
    seq_count = offsets.shape[1] - 1
    per_device = frame_total // seq_count
    capacity = 2 * per_device
    half_width = kernel.shape[0] // 2
    positions = jnp.arange(frame_total, dtype=jnp.int32)
    slot_index = jnp.arange(capacity, dtype=jnp.int32)

    def one_group(carry, inputs):
        rows_in, lens_row, offs_row, cot_rows = inputs
        labels = utterance_of(jnp.arange(-half_width, frame_total + half_width, dtype=jnp.int32), lens_row, frame_total)
        normed, scale_inv = normalize_rows(rows_in)
        hidden = normed.astype(jnp.bfloat16)
        projected = jnp.dot(hidden, w_in, preferred_element_type=jnp.float32)
        values = projected[:, :model_width]
        gates = jax.nn.sigmoid(projected[:, model_width:])
        glu_out = (values * gates).astype(jnp.bfloat16)
        padded = jnp.pad(glu_out, ((half_width, half_width), (0, 0)))
        conv = depthwise(padded, kernel, labels, frame_total)
        conv_normed, conv_inv = normalize_rows(conv)
        gate_out = jax.nn.sigmoid(conv_normed)
        output = conv_normed * gate_out
        output_bf = output.astype(jnp.bfloat16)
        starts = offs_row[:-1]
        loads = offs_row[1:] - starts
        index_rows = jnp.clip(starts[:, None] + slot_index[None, :], 0, frame_total - 1).astype(jnp.int32)
        owned = slot_index[None, :] < loads[:, None]
        owner_rows = jnp.where(owned[:, :, None], output_bf[index_rows], jnp.zeros((), jnp.bfloat16))
        owner_rows = owner_rows.reshape(seq_count * capacity, model_width)
        owner_of = lax.optimization_barrier(jnp.sum((positions[:, None] >= offs_row[None, 1:seq_count]).astype(jnp.int32), axis=1)).astype(jnp.int32)
        slot_of = (owner_of * capacity + positions - offs_row[owner_of]).astype(jnp.int32)
        upstream = cot_rows[slot_of].astype(jnp.float32)
        d_normed = upstream * (gate_out + output * (1.0 - gate_out))
        d_conv = norm_backward(d_normed, conv_normed, conv_inv)
        d_padded = jnp.pad(d_conv, ((half_width, half_width), (0, 0)))
        d_glu = depthwise_back(d_padded, kernel, labels, frame_total)
        d_mixed = jnp.concatenate([d_glu * gates, d_glu * values * gates * (1.0 - gates)], axis=1).astype(jnp.bfloat16)
        d_hidden = jnp.dot(d_mixed, w_in.T, preferred_element_type=jnp.float32)
        d_rows = norm_backward(d_hidden, normed, scale_inv).astype(jnp.bfloat16)

        def block_sum(accumulated, pair):
            hidden_block, mixed_block = pair
            partial_sum = lax.dot_general(hidden_block, mixed_block, (((0,), (0,)), ((), ())), preferred_element_type=jnp.float32)
            partial_sum = lax.optimization_barrier(partial_sum.astype(jnp.bfloat16)).astype(jnp.float32)
            return (accumulated + partial_sum, None)
        carry, unused = lax.scan(block_sum, carry, (hidden.reshape(seq_count, per_device, model_width), d_mixed.reshape(seq_count, per_device, 2 * model_width)))
        return (carry, (owner_rows, d_rows))
    start_sum = jnp.zeros((model_width, 2 * model_width), jnp.float32)
    grad_sum, outputs = lax.scan(one_group, start_sum, (frames, lengths, offsets, cotangent))
    owner_output, frame_grad = outputs
    w_grad = grad_sum * (1.0 / math.sqrt(group_count * frame_total))
    return (owner_output, frame_grad, w_grad)
```

```python
import math

import jax
import jax.numpy as jnp
from jax import lax
from jax.sharding import PartitionSpec as P

epsilon = 1e-05


def passed_along(value, axis, steps):
    count = lax.axis_size(axis)
    initial, last = (max(0, -steps), min(count, count - steps))
    return lax.ppermute(value, axis, [(source, source + steps) for source in range(initial, last)])


def normalize_rows(values):
    values = values.astype(jnp.float32)
    center = jnp.mean(values, axis=-1, keepdims=True)
    shifted = values - center
    scale_inv = lax.rsqrt(jnp.mean(shifted * shifted, axis=-1, keepdims=True) + epsilon)
    return (shifted * scale_inv, scale_inv)


def norm_backward(upstream, normed, scale_inv):
    first_mean = jnp.mean(upstream, axis=-1, keepdims=True)
    second_mean = jnp.mean(upstream * normed, axis=-1, keepdims=True)
    return scale_inv * (upstream - first_mean - normed * second_mean)


def depthwise(window, kernel, labels, row_count):
    tap_count = kernel.shape[0]
    half_width = tap_count // 2
    centre = labels[half_width : half_width + row_count]
    result = jnp.zeros((row_count, kernel.shape[1]), jnp.float32)
    for tap_index in range(tap_count):
        same_utt = (labels[tap_index : tap_index + row_count] == centre).astype(jnp.float32)
        result = (
            result
            + kernel[tap_index]
            * window[tap_index : tap_index + row_count].astype(jnp.float32)
            * same_utt[:, None]
        )
    return result


def depthwise_back(window, kernel, labels, row_count):
    tap_count = kernel.shape[0]
    half_width = tap_count // 2
    centre = labels[half_width : half_width + row_count]
    result = jnp.zeros((row_count, kernel.shape[1]), jnp.float32)
    for tap_index in range(tap_count):
        tap_row = 2 * half_width - tap_index
        same_utt = (labels[tap_row : tap_row + row_count] == centre).astype(jnp.float32)
        result = (
            result + kernel[tap_index] * window[tap_row : tap_row + row_count] * same_utt[:, None]
        )
    return result


def finish(d_glu, values, gates, hidden, normed, scale_inv, backward_product):
    d_mixed = jnp.concatenate(
        [d_glu * gates, d_glu * values * gates * (1.0 - gates)], axis=1
    ).astype(jnp.bfloat16)
    d_hidden = backward_product(d_mixed)
    d_rows = norm_backward(d_hidden, normed, scale_inv).astype(jnp.bfloat16)
    partial_sum = lax.dot_general(
        hidden, d_mixed, (((0,), (0,)), ((), ())), preferred_element_type=jnp.float32
    )
    return (d_rows, partial_sum)


def on_device(frames, lengths, offsets, w_in, kernel, cotangent):
    rows_in = frames[0]
    per_device = rows_in.shape[0]
    model_width = rows_in.shape[1]
    capacity = 2 * per_device
    seq_count = lax.axis_size("seq")
    group_count = lax.axis_size("fsdp")
    device = lax.axis_index("seq")
    frame_total = seq_count * per_device
    half_width = kernel.shape[0] // 2
    bounds_row = offsets[0]
    start_row = bounds_row[device]
    owned_load = bounds_row[device + 1] - start_row
    base_row = (device - 1) * per_device
    first_end = lengths[0, 0]
    second_end = first_end + lengths[0, 1]
    utt_bounds = jnp.stack([first_end, second_end, second_end + lengths[0, 2]])
    slot_index = jnp.arange(capacity, dtype=jnp.int32)
    owned = (slot_index < owned_load)[:, None]
    bf_zero = jnp.zeros((), jnp.bfloat16)
    cot_rows = jnp.where(owned, cotangent[0], bf_zero)

    def backward_product(d_mixed):
        return lax.dot_general(
            d_mixed,
            lax.all_gather(w_in, "fsdp", axis=0, tiled=True),
            (((1,), (1,)), ((), ())),
            preferred_element_type=jnp.float32,
        )

    from_prev = passed_along(rows_in, "seq", 1)
    from_next = passed_along(rows_in, "seq", -1)
    gathered = jnp.concatenate([from_prev, rows_in, from_next, jnp.zeros_like(rows_in)], axis=0)
    window_rows = capacity + 2 * half_width
    rows_window = lax.dynamic_slice_in_dim(
        gathered, start_row - half_width - base_row, window_rows, 0
    )
    positions = start_row - half_width + jnp.arange(window_rows, dtype=jnp.int32)
    labels = jnp.sum((positions[:, None] >= utt_bounds[None, :]).astype(jnp.int32), axis=1)
    inside = (positions >= 0) & (positions < frame_total)
    labels = jnp.where(inside, labels, -1)
    normed, scale_inv = normalize_rows(rows_window)
    hidden = normed.astype(jnp.bfloat16)
    projected = jnp.dot(
        hidden, lax.all_gather(w_in, "fsdp", axis=0, tiled=True), preferred_element_type=jnp.float32
    )
    values = projected[:, :model_width]
    gates = jax.nn.sigmoid(projected[:, model_width:])
    glu_out = (values * gates).astype(jnp.bfloat16)
    conv = depthwise(glu_out, kernel, labels, capacity)
    conv_normed, conv_inv = normalize_rows(conv)
    gate_out = jax.nn.sigmoid(conv_normed)
    output = conv_normed * gate_out
    owner_output = jnp.where(owned, output.astype(jnp.bfloat16), bf_zero)
    upstream = cot_rows.astype(jnp.float32)
    d_normed = upstream * (gate_out + output * (1.0 - gate_out))
    d_conv = jnp.where(owned, norm_backward(d_normed, conv_normed, conv_inv), 0.0)
    tail_rows = lax.dynamic_slice_in_dim(d_conv, owned_load - half_width, half_width, 0)
    head_rows = d_conv[:half_width]
    left_part = passed_along(tail_rows.astype(jnp.bfloat16), "seq", 1).astype(tail_rows.dtype)
    right_part = passed_along(head_rows.astype(jnp.bfloat16), "seq", -1).astype(head_rows.dtype)
    edge_zeros = jnp.zeros((half_width, model_width), jnp.float32)
    d_window = jnp.concatenate([left_part, d_conv, edge_zeros], axis=0)
    right_placed = lax.dynamic_update_slice_in_dim(
        jnp.zeros((window_rows, model_width), jnp.float32), right_part, half_width + owned_load, 0
    )
    d_window = d_window + right_placed
    d_glu = jnp.where(owned, depthwise_back(d_window, kernel, labels, capacity), 0.0)
    inner_end = half_width + capacity
    d_rows, partial_sum = finish(
        d_glu,
        values[half_width:inner_end],
        gates[half_width:inner_end],
        hidden[half_width:inner_end],
        normed[half_width:inner_end],
        scale_inv[half_width:inner_end],
        backward_product,
    )
    placed = lax.dynamic_update_slice_in_dim(
        jnp.zeros((4 * per_device, model_width), jnp.bfloat16), d_rows, start_row - base_row, 0
    )
    back_prev = passed_along(placed[:per_device], "seq", -1)
    back_next = passed_along(placed[2 * per_device : 3 * per_device], "seq", 1)
    frame_grad = (
        placed[per_device : 2 * per_device].astype(jnp.float32)
        + back_prev.astype(jnp.float32)
        + back_next.astype(jnp.float32)
    ).astype(jnp.bfloat16)
    rounded = lax.optimization_barrier(partial_sum.astype(jnp.bfloat16)).astype(jnp.float32)
    seq_summed = lax.psum_scatter(
        rounded.astype(jnp.bfloat16), "seq", scatter_dimension=0, tiled=True
    )
    summed = lax.psum_scatter(seq_summed, "fsdp", scatter_dimension=0, tiled=True).astype(
        jnp.float32
    )
    w_grad = summed * (1.0 / math.sqrt(group_count * frame_total))
    return (owner_output[None], frame_grad[None], w_grad)


def solution(mesh):
    return jax.shard_map(
        on_device,
        mesh=mesh,
        in_specs=(
            P("fsdp", "seq", None),
            P("fsdp", None),
            P("fsdp", None),
            P("fsdp", None),
            P(),
            P("fsdp", "seq", None),
        ),
        out_specs=(P("fsdp", "seq", None), P("fsdp", "seq", None), P(("seq", "fsdp"), None)),
        check_vma=False,
    )
```

```python
import functools
import math

import jax
import jax.numpy as jnp
from jax import lax
from jax.experimental import pallas as pl
from jax.experimental.pallas import tpu as pltpu
from jax.sharding import PartitionSpec as P

epsilon = 1e-05
bf16 = jnp.bfloat16
f32 = jnp.float32
LANES = 128
BLOCK = 32
SEQ = ("x", "z")
CHIP = 2
NEAR = 3


def passed_along(value, axis, steps):
    count = lax.axis_size(axis)
    initial, last = (max(0, -steps), min(count, count - steps))
    return lax.ppermute(value, axis, [(source, source + steps) for source in range(initial, last)])


def normalize_rows(values):
    values = values.astype(f32)
    center = jnp.mean(values, axis=-1, keepdims=True)
    shifted = values - center
    scale_inv = lax.rsqrt(jnp.mean(shifted * shifted, axis=-1, keepdims=True) + epsilon)
    return (shifted * scale_inv, scale_inv)


def shifted_copies(source, copies, rows):
    copies[0, :rows] = source
    for shift in range(1, 8):
        copies[shift, :rows] = pltpu.roll(source, rows - shift, 0)


def tap_sum(copies, mask_ref, ker_ref, lanes, row, mask_row, count, flip, masked):
    tap_count = ker_ref.shape[0]
    total = jnp.zeros((count, LANES), f32)
    for tap in range(tap_count):
        tile, shift = divmod(tap + 1, 8)
        weight = ker_ref[pl.ds(tap_count - 1 - tap if flip else tap, 1), lanes]
        term = weight * copies[shift, pl.ds(row + 8 * tile, count), :]
        if masked:
            term = term * mask_ref[tap, pl.ds(mask_row, count), :]
        total = total + term
    return total


def centred(values):
    inverse = 1.0 / values.shape[-1]
    center = jnp.sum(values, axis=-1, keepdims=True) * inverse
    shifted = values - center
    variance = jnp.sum(shifted * shifted, axis=-1, keepdims=True) * inverse
    scale_inv = lax.rsqrt(variance + epsilon)
    return shifted * scale_inv, scale_inv


def started(copies):
    for copy in copies:
        copy.start()
    return copies


def pair_copies(core_ref, pieces, target, sem, first):
    copies = []
    half = len(pieces) // 2
    rows = target.shape[0] // CHIP
    for index, piece in enumerate(pieces):
        count = piece.shape[0]
        core = core_ref[0] if index < half else 1 - core_ref[0]
        start = pl.multiple_of(core * rows + (index % half) * count, 16)
        copies.append(
            pltpu.make_async_copy(piece, target.at[pl.ds(start, count), :], sem.at[first + index])
        )
    return copies


def chip_copies(core_ref, pieces, w_buf, sem):
    copies = []
    first = 0
    for chip in range(w_buf.shape[0]):
        count = 2 if chip < NEAR else 4
        copies.append(pair_copies(core_ref, pieces[first : first + count], w_buf.at[chip], sem, first))
        first += count
    return copies


def part_kernel(halo, at_ref, core_ref, prev_ref, rows_ref, next_ref, *rest):
    piece_count = len(rest) - 4
    pieces = rest[:piece_count]
    hid_ref, part_ref, w_buf, sem = rest[piece_count:]
    chips = w_buf.shape[0]
    depth = w_buf.shape[1]
    copies = chip_copies(core_ref, pieces, w_buf, sem)
    for chip in range(chips):
        started(copies[chip])

    def normalize(source, first, count, target):
        @pl.loop(0, count // 16)
        def _(block):
            taken = pl.ds(pl.multiple_of(first + block * 16, 16), 16)
            put = pl.ds(pl.multiple_of(target + block * 16, 16), 16)
            hid_ref[put, :] = centred(source[taken, :].astype(f32))[0].astype(bf16)

    rows = rows_ref.shape[0]
    normalize(prev_ref, 0, halo, 0)
    normalize(rows_ref, 0, rows, halo)
    normalize(next_ref, next_ref.shape[0] - halo, halo, halo + rows)

    for chip in range(chips):
        for copy in copies[chip]:
            copy.wait()

    @pl.loop(0, part_ref.shape[1] // 256)
    def _(block):
        at = pl.ds(pl.multiple_of(block * 256, 256), 256)
        total = jnp.zeros((hid_ref.shape[0], 256), f32)
        for chip in range(chips):
            lanes = pl.ds(pl.multiple_of(at_ref[chip] * depth, LANES), depth)
            total = total + jnp.dot(
                hid_ref[:, lanes], w_buf[chip, :, at], preferred_element_type=f32
            )
        part_ref[:, at] = total


def main_kernel(rows, edge, bounds_ref, at_ref, core_ref, hid_ref, part_ref, up_ref, ker_ref, *rest):
    piece_count = len(rest) - 11
    pieces = rest[:piece_count]
    out_ref, dm_ref, shares_ref, w_buf, val, gate, glu, conv, copies_buf, mask_ref, sem = rest[piece_count:]
    width = hid_ref.shape[1]
    window = rows + 4 * edge
    wide = rows + 2 * edge
    tap_count = ker_ref.shape[0]
    half_width = tap_count // 2
    copies = started(pair_copies(core_ref, pieces, w_buf, sem, 0))
    depth = w_buf.shape[0]
    far = pl.ds(pl.multiple_of(at_ref[at_ref.shape[0] - 1] * depth, LANES), depth)
    base = bounds_ref[0]
    last = bounds_ref[1]
    ends = [bounds_ref[index] for index in range(2, bounds_ref.shape[0])]

    def crossed(first, count):
        found = jnp.bool_(False)
        for end in ends:
            found = found | ((end > first - half_width) & (end < first + count + half_width))
        return found

    @pl.when(crossed(base, wide))
    def _():
        @pl.loop(0, wide // 8)
        def _(block):
            row = pl.multiple_of(block * 8, 8)
            position = base + row + lax.broadcasted_iota(jnp.int32, (8, LANES), 0)
            low = jnp.zeros((8, LANES), jnp.int32)
            high = jnp.full((8, LANES), last, jnp.int32)
            for end in ends:
                low = jnp.where(position >= end, jnp.maximum(low, end), low)
                high = jnp.where(position < end, jnp.minimum(high, end), high)
            low = low - position + half_width
            high = high - position + half_width
            for tap in range(tap_count):
                mask_ref[tap, pl.ds(row, 8), :] = jnp.where((low <= tap) & (high > tap), 1.0, 0.0).astype(f32)

    for copy in copies:
        copy.wait()

    @pl.loop(0, width // 256)
    def _(block):
        at = pl.ds(pl.multiple_of(block * 256, 256), 256)
        gate_at = pl.ds(pl.multiple_of(block * 256 + width, 256), 256)
        values = part_ref[:, at] + jnp.dot(hid_ref[:, far], w_buf[:, at], preferred_element_type=f32)
        gates = jax.nn.sigmoid(
            part_ref[:, gate_at]
            + jnp.dot(hid_ref[:, far], w_buf[:, gate_at], preferred_element_type=f32)
        )
        val[:, at] = values[2 * edge : 2 * edge + rows]
        gate[:, at] = gates[2 * edge : 2 * edge + rows]
        glu[:, at] = (values * gates).astype(bf16).astype(f32)

    @pl.loop(0, width // LANES)
    def _(block):
        lanes = pl.ds(pl.multiple_of(block * LANES, LANES), LANES)
        shifted_copies(glu[:, lanes], copies_buf, window)

        @pl.loop(0, wide // BLOCK)
        def _(step):
            row = pl.multiple_of(step * BLOCK, BLOCK)
            cut = crossed(base + row, BLOCK)

            @pl.when(jnp.logical_not(cut))
            def _():
                conv[pl.ds(row, BLOCK), lanes] = tap_sum(
                    copies_buf, mask_ref, ker_ref, lanes, row, row, BLOCK, False, False
                )

            @pl.when(cut)
            def _():
                conv[pl.ds(row, BLOCK), lanes] = tap_sum(
                    copies_buf, mask_ref, ker_ref, lanes, row, row, BLOCK, False, True
                )

    @pl.loop(0, wide // 16)
    def _(block):
        at = pl.ds(pl.multiple_of(block * 16, 16), 16)
        normed, scale_inv = centred(conv[at, :])
        gates = jax.nn.sigmoid(normed)
        output = normed * gates

        @pl.when((block >= edge // 16) & (block < (edge + rows) // 16))
        def _():
            out_ref[pl.ds(pl.multiple_of(block * 16 - edge, 16), 16), :] = output.astype(bf16)

        d_normed = up_ref[at, :].astype(f32) * (gates + output * (1.0 - gates))
        conv[at, :] = back_through_norm(d_normed, normed, scale_inv)

    @pl.loop(0, width // LANES)
    def _(block):
        lanes = pl.ds(pl.multiple_of(block * LANES, LANES), LANES)
        gate_lanes = pl.ds(pl.multiple_of(block * LANES + width, LANES), LANES)
        shifted_copies(conv[:, lanes], copies_buf, wide)
        per_share = shares_ref.shape[2] // LANES
        share = lax.div(block, per_share)
        share_lanes = pl.ds(pl.multiple_of((block - share * per_share) * LANES, LANES), LANES)

        @pl.loop(0, rows // BLOCK)
        def _(step):
            row = pl.multiple_of(step * BLOCK, BLOCK)
            at = pl.ds(row, BLOCK)
            cut = crossed(base + edge + row, BLOCK)

            def finish(masked):
                d_glu = tap_sum(
                    copies_buf, mask_ref, ker_ref, lanes, row, row + edge, BLOCK, True, masked
                )
                gates = gate[at, lanes]
                d_values = d_glu * gates
                d_gates = (d_values * val[at, lanes] * (1.0 - gates)).astype(bf16)
                d_values = d_values.astype(bf16)
                dm_ref[at, lanes] = d_values
                dm_ref[at, gate_lanes] = d_gates
                shares_ref[share, at, share_lanes] = d_values
                shares_ref[share + shares_ref.shape[0] // 2, at, share_lanes] = d_gates

            @pl.when(jnp.logical_not(cut))
            def _():
                finish(False)

            @pl.when(cut)
            def _():
                finish(True)


def back_through_norm(upstream, normed, scale_inv):
    inverse = 1.0 / normed.shape[-1]
    first_mean = jnp.sum(upstream, axis=-1, keepdims=True) * inverse
    second_mean = jnp.sum(upstream * normed, axis=-1, keepdims=True) * inverse
    return scale_inv * (upstream - first_mean - normed * second_mean)


def frame_kernel(at_ref, core_ref, rows_ref, dm_ref, *rest):
    piece_count = len(rest) - 4
    pieces = rest[:piece_count]
    grad_ref, w_buf, d_hidden, sem = rest[piece_count:]
    rows, width = rows_ref.shape
    chips, depth = w_buf.shape[:2]
    copies = chip_copies(core_ref, pieces, w_buf, sem)
    for chip in range(chips):
        started(copies[chip])
    for chip in range(chips):
        for copy in copies[chip]:
            copy.wait()
        lanes = pl.ds(pl.multiple_of(at_ref[chip] * depth, LANES), depth)
        d_hidden[:, lanes] = lax.dot_general(
            dm_ref[...], w_buf[chip], (((1,), (1,)), ((), ())), preferred_element_type=f32
        )

    @pl.loop(0, rows // 16)
    def _(block):
        at = pl.ds(pl.multiple_of(block * 16, 16), 16)
        normed, scale_inv = centred(rows_ref[at, :].astype(f32))
        grad_ref[at, :] = back_through_norm(d_hidden[at, :], normed, scale_inv).astype(bf16)


VMEM = pl.BlockSpec(memory_space=pltpu.VMEM)
SMEM = pl.BlockSpec(memory_space=pltpu.SMEM)
ANY = pl.BlockSpec(memory_space=pltpu.HBM)


def limit(mib):
    return pltpu.CompilerParams(vmem_limit_bytes=mib * 1024 * 1024)


def run_part(chips, core, from_prev, rows_in, from_next, pieces, halo):
    rows, width = rows_in.shape
    big = rows + 2 * halo
    depth = pieces[0].shape[0] * CHIP
    mixed_width = pieces[0].shape[1]
    return pl.pallas_call(
        functools.partial(part_kernel, halo),
        out_shape=(
            jax.ShapeDtypeStruct((big, width), bf16),
            jax.ShapeDtypeStruct((big, mixed_width), f32),
        ),
        in_specs=[SMEM, SMEM, VMEM, VMEM, VMEM] + [ANY] * len(pieces),
        out_specs=(VMEM, VMEM),
        scratch_shapes=[
            pltpu.VMEM((chips.shape[0], depth, mixed_width), bf16),
            pltpu.SemaphoreType.DMA((len(pieces),)),
        ],
        compiler_params=limit(44),
        cost_estimate=pl.CostEstimate(flops=2 * 10**9, bytes_accessed=8 * 10**6, transcendentals=0),
        name="forward_part",
    )(chips, core, from_prev, rows_in, from_next, *pieces)


def run_main(bounds, chips, core, hidden, part, upstream, kernel, pieces, rows, edge, shares):
    big, width = hidden.shape
    wide = upstream.shape[0]
    taps = kernel.shape[0]
    depth = sum(piece.shape[0] for piece in pieces)
    return pl.pallas_call(
        functools.partial(main_kernel, rows, edge),
        out_shape=(
            jax.ShapeDtypeStruct((rows, width), bf16),
            jax.ShapeDtypeStruct((rows, 2 * width), bf16),
            jax.ShapeDtypeStruct((shares, rows, 2 * width // shares), bf16),
        ),
        in_specs=[SMEM, SMEM, SMEM, VMEM, VMEM, VMEM, VMEM] + [ANY] * len(pieces),
        out_specs=(VMEM, VMEM, VMEM),
        scratch_shapes=[
            pltpu.VMEM((depth, 2 * width), bf16),
            pltpu.VMEM((rows, width), f32),
            pltpu.VMEM((rows, width), f32),
            pltpu.VMEM((big, width), f32),
            pltpu.VMEM((wide, width), f32),
            pltpu.VMEM((8, big, LANES), f32),
            pltpu.VMEM((taps, wide, LANES), f32),
            pltpu.SemaphoreType.DMA((len(pieces),)),
        ],
        compiler_params=limit(44),
        cost_estimate=pl.CostEstimate(flops=6 * 10**9, bytes_accessed=12 * 10**6, transcendentals=0),
        name="main",
    )(bounds, chips, core, hidden, part, upstream, kernel, *pieces)


def run_frame(chips, core, rows_in, d_mixed, pieces):
    rows, width = rows_in.shape
    return pl.pallas_call(
        frame_kernel,
        out_shape=jax.ShapeDtypeStruct((rows, width), bf16),
        in_specs=[SMEM, SMEM, VMEM, VMEM] + [ANY] * len(pieces),
        out_specs=VMEM,
        scratch_shapes=[
            pltpu.VMEM((chips.shape[0], width // chips.shape[0], 2 * width), bf16),
            pltpu.VMEM((rows, width), f32),
            pltpu.SemaphoreType.DMA((len(pieces),)),
        ],
        compiler_params=limit(58),
        cost_estimate=pl.CostEstimate(flops=2 * 10**9, bytes_accessed=11 * 10**6, transcendentals=0),
        name="frame_back",
    )(chips, core, rows_in, d_mixed, *pieces)


def ring(value, axis, steps):
    count = lax.axis_size(axis)
    return lax.ppermute(value, axis, [(i, (i + steps) % count) for i in range(count)])


def other_core(value):
    return lax.ppermute(value, "c", [(0, 1), (1, 0)])


def weight_blocks(w_in):
    half = w_in.shape[0] // 2
    below, above = ring(w_in, "y", 1), ring(w_in, "y", -1)
    return below, above, [ring(below[:half], "y", 1), ring(above[half:], "y", -1)]


def exchange_edges(rows_in, cot_rows, bounds_row, device, edge):
    rows, width = rows_in.shape
    halo = 2 * edge
    sent = rows // 2 + edge
    load = bounds_row[device + 1] - bounds_row[device]
    slot = jnp.arange(cot_rows.shape[0], dtype=jnp.int32)[:, None]
    own = jnp.where(slot < load, cot_rows, jnp.zeros((), cot_rows.dtype))
    padded = jnp.concatenate([jnp.zeros((sent, width), own.dtype), own], axis=0)
    last_rows = lax.dynamic_slice_in_dim(padded, load, sent, 0)
    upwards = jnp.concatenate([rows_in[rows - halo :], last_rows], axis=0)
    downwards = jnp.concatenate([own[:sent], rows_in[:halo]], axis=0)
    return own, passed_along(upwards, SEQ, 1), passed_along(downwards, SEQ, -1)


def upstream_window(own, from_prev, from_next, bounds_row, device, rows, edge):
    came, width = from_prev.shape
    start_row = bounds_row[device]
    load = bounds_row[device + 1] - start_row
    joined = jnp.concatenate([from_prev, own, jnp.zeros((came, width), own.dtype)], axis=0)
    joined = lax.dynamic_update_slice_in_dim(joined, from_next, came + load, 0)
    first = rows * device - edge - (start_row - came)
    return lax.dynamic_slice_in_dim(joined, first, rows + 2 * edge, 0)


def owner_slots(out_rows, bounds_row, device):
    rows, width = out_rows.shape
    half = rows // 2
    from_prev = passed_along(out_rows[half:], SEQ, 1)
    from_next = passed_along(out_rows[:half], SEQ, -1)
    start_row = bounds_row[device]
    load = bounds_row[device + 1] - start_row
    joined = jnp.concatenate(
        [from_prev, out_rows, from_next, jnp.zeros((rows, width), out_rows.dtype)], axis=0
    )
    placed = lax.dynamic_slice_in_dim(joined, start_row - (rows * device - half), 2 * rows, 0)
    slot = jnp.arange(2 * rows, dtype=jnp.int32)[:, None]
    return jnp.where(slot < load, placed, jnp.zeros((), placed.dtype))


def by_receiver(hidden):
    width = hidden.shape[1]
    xs, zs, ys = lax.axis_size("x"), lax.axis_size("z"), lax.axis_size("y")
    kept = width // (xs * zs * ys)
    place = jnp.arange(width, dtype=jnp.int32)
    rest, row = place // kept, place % kept
    x, rest = rest % xs, rest // xs
    z, y = rest % zs, rest // zs
    feature = ((x * zs + z) * ys + y) * kept + row
    chosen = (place[:, None] == feature[None, :]).astype(bf16)
    return jnp.dot(hidden, chosen, preferred_element_type=f32).astype(bf16)


def hidden_blocks(hidden):
    return [ring(hidden, "x", -1), ring(hidden, "x", 2), ring(hidden, "x", 1), hidden]


def all_hidden(blocks):
    count = lax.axis_size("x")
    blocks = jnp.stack(blocks)
    others = other_core(blocks)
    core = lax.axis_index("c")
    both = jnp.stack(
        [jnp.where(core == 0, blocks, others), jnp.where(core == 0, others, blocks)], axis=1
    )
    twice = jnp.concatenate([both, both], axis=0)
    first = (count - 1 - lax.axis_index("x")) % count
    ordered = lax.dynamic_slice_in_dim(twice, first, count, 0)
    return ordered.reshape(-1, blocks.shape[-1])


def weight_gradient(hidden_all, mixed_share, frame_total, group_count):
    width = hidden_all.shape[1]
    share = mixed_share.shape[1]
    ys = lax.axis_size("y")
    y = lax.axis_index("y")
    taken = width // ys

    def product(steps):
        columns = lax.dynamic_slice_in_dim(hidden_all, taken * ((y + steps) % ys), taken, 1)
        return lax.dot_general(
            columns, mixed_share, (((0,), (0,)), ((), ())), preferred_element_type=f32
        )

    from_far = ring(product(2).astype(bf16), "y", 2).astype(f32)
    from_below = ring(product(1).astype(bf16), "y", 1).astype(f32)
    from_above = ring(product(3).astype(bf16), "y", -1).astype(f32)
    own, from_far = lax.optimization_barrier((product(0), from_far))
    summed = (own + from_far + from_below + from_above).astype(bf16)
    last = ("z", "x", "c")
    receivers = lax.axis_size(last)
    pieces = summed.reshape(receivers, taken // receivers, share)
    pieces = lax.all_to_all(pieces, last, 0, 0, tiled=True).astype(f32)
    pieces = jnp.sum(pieces.reshape(lax.axis_size("z"), -1, taken // receivers, share), axis=0)
    w_grad = jnp.swapaxes(pieces, 0, 1).reshape(taken // receivers, -1)
    return w_grad * (1.0 / math.sqrt(group_count * frame_total))


def on_device(frames, lengths, offsets, w_in, kernel, cotangent):
    rows_in = frames[0]
    rows, width = rows_in.shape
    half_width = kernel.shape[0] // 2
    edge = half_width + 1
    halo = 2 * edge
    seq_count = lax.axis_size(SEQ)
    device = lax.axis_index(SEQ)
    frame_total = seq_count * rows
    bounds_row = offsets[0]
    chip = lax.axis_index("y")
    chips = lax.axis_size("y")
    core = lax.axis_index("c").reshape(1)
    below, above, far = weight_blocks(w_in)
    own_other = other_core(w_in)
    own, from_prev, from_next = exchange_edges(
        rows_in, cotangent[0], bounds_row, device, edge
    )
    upstream = upstream_window(own, from_prev, from_next, bounds_row, device, rows, edge)
    rows_late, own_other = lax.optimization_barrier((rows_in, own_other))
    near = [w_in, own_other, below, other_core(below), above, other_core(above)]
    order = jnp.stack([chip, (chip + chips - 1) % chips, (chip + 1) % chips, (chip + 2) % chips])

    hidden_sent = by_receiver(normalize_rows(rows_late)[0].astype(bf16))
    hidden_sent, _, _ = lax.optimization_barrier(
        (hidden_sent, from_prev[:8, :LANES], from_next[:8, :LANES])
    )
    blocks = hidden_blocks(hidden_sent)

    bounds = [rows * device - edge, jnp.int32(frame_total)]
    utt_end = jnp.int32(0)
    for utt in range(lengths.shape[1] - 1):
        utt_end = utt_end + lengths[0, utt]
        bounds.append(utt_end)
    bounds = jnp.stack(bounds).astype(jnp.int32)

    hidden, part = run_part(order[:3], core, from_prev, rows_in, from_next, near, halo)
    far, _, _ = lax.optimization_barrier((far, upstream[:8, :LANES], part[:8, :LANES]))
    far = far + [other_core(piece) for piece in far]
    shares = lax.axis_size(("x", "c"))
    output, d_mixed, d_shares = run_main(
        bounds, order, core, hidden, part, upstream, kernel, far, rows, edge, shares
    )
    blocks, d_shares = lax.optimization_barrier((blocks, d_shares))
    hidden_all = all_hidden(blocks)
    mixed_share = lax.all_to_all(d_shares, ("x", "c"), 0, 0, tiled=True)
    mixed_share = mixed_share.reshape(shares * rows, -1)
    frame_grad = run_frame(order, core, rows_in, d_mixed, near + far)
    w_grad = weight_gradient(hidden_all, mixed_share, frame_total, chips * CHIP)
    owner_output = owner_slots(output, bounds_row, device)
    return (owner_output[None], frame_grad[None], w_grad)


def solution(mesh):
    seq_count, group_count = mesh.devices.shape
    ys, xs = group_count // CHIP, 4
    devices = mesh.devices.reshape(xs, seq_count // xs, ys, CHIP)
    groups = ("y", "c")
    return jax.shard_map(
        on_device,
        mesh=jax.sharding.Mesh(devices, ("x", "z", "y", "c")),
        in_specs=(
            P(groups, SEQ, None),
            P(groups, None),
            P(groups, None),
            P(groups, None),
            P(),
            P(groups, SEQ, None),
        ),
        out_specs=(P(groups, SEQ, None), P(groups, SEQ, None), P((*SEQ, *groups), None)),
        check_vma=False,
    )
```

```python
import functools
import math

import jax
import jax.numpy as jnp
from jax import lax
from jax.experimental import pallas as pl
from jax.experimental.pallas import tpu as pltpu
from jax.sharding import PartitionSpec as P

epsilon = 1e-05
bf16 = jnp.bfloat16
f32 = jnp.float32
LANES = 128
BLOCK = 32
SEQ = ("x", "z")
CHIP = 2
NEAR = 3


def passed_along(value, axis, steps):
    count = lax.axis_size(axis)
    initial, last = (max(0, -steps), min(count, count - steps))
    return lax.ppermute(value, axis, [(source, source + steps) for source in range(initial, last)])


def normalize_rows(values):
    values = values.astype(f32)
    center = jnp.mean(values, axis=-1, keepdims=True)
    shifted = values - center
    scale_inv = lax.rsqrt(jnp.mean(shifted * shifted, axis=-1, keepdims=True) + epsilon)
    return (shifted * scale_inv, scale_inv)


def shifted_copies(source, copies, rows):
    copies[0, :rows] = source
    for shift in range(1, 8):
        copies[shift, :rows] = pltpu.roll(source, rows - shift, 0)


def tap_sum(copies, mask_ref, ker_ref, lanes, row, mask_row, count, flip, masked):
    tap_count = ker_ref.shape[0]
    totals = [jnp.zeros((count, LANES), f32)] * 2
    for tap in range(tap_count):
        tile, shift = divmod(tap + 1, 8)
        weight = ker_ref[pl.ds(tap_count - 1 - tap if flip else tap, 1), lanes]
        term = weight * copies[shift, pl.ds(row + 8 * tile, count), :]
        if masked:
            term = term * mask_ref[tap, pl.ds(mask_row, count), :]
        totals[tap % 2] = totals[tap % 2] + term
    return totals[0] + totals[1]


def centred(values):
    inverse = 1.0 / values.shape[-1]
    center = jnp.sum(values, axis=-1, keepdims=True) * inverse
    shifted = values - center
    variance = jnp.sum(shifted * shifted, axis=-1, keepdims=True) * inverse
    scale_inv = lax.rsqrt(variance + epsilon)
    return shifted * scale_inv, scale_inv


def started(copies):
    for copy in copies:
        copy.start()
    return copies


def pair_copies(core_ref, pieces, target, sem, first):
    copies = []
    half = len(pieces) // 2
    rows = target.shape[0] // CHIP
    for index, piece in enumerate(pieces):
        count = piece.shape[0]
        core = core_ref[0] if index < half else 1 - core_ref[0]
        start = pl.multiple_of(core * rows + (index % half) * count, 16)
        copies.append(
            pltpu.make_async_copy(piece, target.at[pl.ds(start, count), :], sem.at[first + index])
        )
    return copies


def chip_copies(core_ref, pieces, w_buf, sem):
    copies = []
    first = 0
    for chip in range(w_buf.shape[0]):
        count = 2 if chip < NEAR else 4
        copies.append(pair_copies(core_ref, pieces[first : first + count], w_buf.at[chip], sem, first))
        first += count
    return copies


def part_kernel(halo, at_ref, core_ref, prev_ref, rows_ref, next_ref, *rest):
    piece_count = len(rest) - 4
    pieces = rest[:piece_count]
    hid_ref, part_ref, w_buf, sem = rest[piece_count:]
    chips = w_buf.shape[0]
    depth = w_buf.shape[1]
    copies = chip_copies(core_ref, pieces, w_buf, sem)
    for chip in range(chips):
        started(copies[chip])

    def normalize(source, first, count, target):
        @pl.loop(0, count // 16)
        def _(block):
            taken = pl.ds(pl.multiple_of(first + block * 16, 16), 16)
            put = pl.ds(pl.multiple_of(target + block * 16, 16), 16)
            hid_ref[put, :] = centred(source[taken, :].astype(f32))[0].astype(bf16)

    rows = rows_ref.shape[0]
    normalize(prev_ref, 0, halo, 0)
    normalize(rows_ref, 0, rows, halo)
    normalize(next_ref, next_ref.shape[0] - halo, halo, halo + rows)

    for chip in range(chips):
        for copy in copies[chip]:
            copy.wait()

    @pl.loop(0, part_ref.shape[1] // 256)
    def _(block):
        at = pl.ds(pl.multiple_of(block * 256, 256), 256)
        total = jnp.zeros((hid_ref.shape[0], 256), f32)
        for chip in range(chips):
            lanes = pl.ds(pl.multiple_of(at_ref[chip] * depth, LANES), depth)
            total = total + jnp.dot(
                hid_ref[:, lanes], w_buf[chip, :, at], preferred_element_type=f32
            )
        part_ref[:, at] = total


def main_kernel(rows, edge, bounds_ref, at_ref, core_ref, corner_ref, hid_ref, part_ref, up_ref, ker_ref, *rest):
    piece_count = len(rest) - 11
    pieces = rest[:piece_count]
    out_ref, dm_ref, shares_ref, w_buf, val, gate, glu, conv, copies_buf, mask_ref, sem = rest[piece_count:]
    width = hid_ref.shape[1]
    window = rows + 4 * edge
    wide = rows + 2 * edge
    tap_count = ker_ref.shape[0]
    half_width = tap_count // 2
    copies = started(pair_copies(core_ref, pieces, w_buf, sem, 0))
    depth = w_buf.shape[0]
    far = pl.ds(pl.multiple_of(at_ref[at_ref.shape[0] - 1] * depth, LANES), depth)
    base = bounds_ref[0]
    last = bounds_ref[1]
    ends = [bounds_ref[index] for index in range(2, bounds_ref.shape[0])]

    def crossed(first, count):
        found = jnp.bool_(False)
        for end in ends:
            found = found | ((end > first - half_width) & (end < first + count + half_width))
        return found

    @pl.when(crossed(base, wide))
    def _():
        @pl.loop(0, wide // 8)
        def _(block):
            row = pl.multiple_of(block * 8, 8)
            position = base + row + lax.broadcasted_iota(jnp.int32, (8, LANES), 0)
            low = jnp.zeros((8, LANES), jnp.int32)
            high = jnp.full((8, LANES), last, jnp.int32)
            for end in ends:
                low = jnp.where(position >= end, jnp.maximum(low, end), low)
                high = jnp.where(position < end, jnp.minimum(high, end), high)
            low = low - position + half_width
            high = high - position + half_width
            for tap in range(tap_count):
                mask_ref[tap, pl.ds(row, 8), :] = jnp.where((low <= tap) & (high > tap), 1.0, 0.0).astype(f32)

    for copy in copies:
        copy.wait()

    @pl.loop(0, width // 256)
    def _(block):
        at = pl.ds(pl.multiple_of(block * 256, 256), 256)
        gate_at = pl.ds(pl.multiple_of(block * 256 + width, 256), 256)
        values = part_ref[:, at] + jnp.dot(hid_ref[:, far], w_buf[:, at], preferred_element_type=f32)
        gates = jax.nn.sigmoid(
            part_ref[:, gate_at]
            + jnp.dot(hid_ref[:, far], w_buf[:, gate_at], preferred_element_type=f32)
        )
        val[:, at] = values[2 * edge : 2 * edge + rows]
        gate[:, at] = gates[2 * edge : 2 * edge + rows]
        glu[:, at] = (values * gates).astype(bf16).astype(f32)

    @pl.loop(0, width // LANES)
    def _(block):
        lanes = pl.ds(pl.multiple_of(block * LANES, LANES), LANES)
        shifted_copies(glu[:, lanes], copies_buf, window)

        @pl.loop(0, wide // BLOCK)
        def _(step):
            row = pl.multiple_of(step * BLOCK, BLOCK)
            cut = crossed(base + row, BLOCK)

            @pl.when(jnp.logical_not(cut))
            def _():
                conv[pl.ds(row, BLOCK), lanes] = tap_sum(
                    copies_buf, mask_ref, ker_ref, lanes, row, row, BLOCK, False, False
                )

            @pl.when(cut)
            def _():
                conv[pl.ds(row, BLOCK), lanes] = tap_sum(
                    copies_buf, mask_ref, ker_ref, lanes, row, row, BLOCK, False, True
                )

    @pl.loop(0, wide // 16)
    def _(block):
        at = pl.ds(pl.multiple_of(block * 16, 16), 16)
        normed, scale_inv = centred(conv[at, :])
        gates = jax.nn.sigmoid(normed)
        output = normed * gates

        @pl.when((block >= edge // 16) & (block < (edge + rows) // 16))
        def _():
            out_ref[pl.ds(pl.multiple_of(block * 16 - edge, 16), 16), :] = output.astype(bf16)

        d_normed = up_ref[at, :].astype(f32) * (gates + output * (1.0 - gates))
        conv[at, :] = back_through_norm(d_normed, normed, scale_inv)

    @pl.loop(0, width // LANES)
    def _(block):
        lanes = pl.ds(pl.multiple_of(block * LANES, LANES), LANES)
        gate_lanes = pl.ds(pl.multiple_of(block * LANES + width, LANES), LANES)
        shifted_copies(conv[:, lanes], copies_buf, wide)
        per_share = shares_ref.shape[2] // LANES
        share = lax.div(block, per_share)
        share_lanes = pl.ds(pl.multiple_of((block - share * per_share) * LANES, LANES), LANES)

        @pl.loop(0, rows // BLOCK)
        def _(step):
            row = pl.multiple_of(step * BLOCK, BLOCK)
            at = pl.ds(row, BLOCK)
            cut = crossed(base + edge + row, BLOCK)

            def finish(masked):
                d_glu = tap_sum(
                    copies_buf, mask_ref, ker_ref, lanes, row, row + edge, BLOCK, True, masked
                )
                gates = gate[at, lanes]
                d_values = d_glu * gates
                d_gates = (d_values * val[at, lanes] * (1.0 - gates)).astype(bf16)
                d_values = d_values.astype(bf16)
                dm_ref[at, lanes] = d_values
                dm_ref[at, gate_lanes] = d_gates
                shares_ref[share, at, share_lanes] = d_values
                shares_ref[share + shares_ref.shape[0] // 2, at, share_lanes] = d_gates

            @pl.when(jnp.logical_not(cut))
            def _():
                finish(False)

            @pl.when(cut)
            def _():
                finish(True)


def back_through_norm(upstream, normed, scale_inv):
    inverse = 1.0 / normed.shape[-1]
    first_mean = jnp.sum(upstream, axis=-1, keepdims=True) * inverse
    second_mean = jnp.sum(upstream * normed, axis=-1, keepdims=True) * inverse
    return scale_inv * (upstream - first_mean - normed * second_mean)


def frame_kernel(at_ref, core_ref, rows_ref, dm_ref, *rest):
    piece_count = len(rest) - 4
    pieces = rest[:piece_count]
    grad_ref, w_buf, d_hidden, sem = rest[piece_count:]
    rows, width = rows_ref.shape
    chips, depth = w_buf.shape[:2]
    copies = chip_copies(core_ref, pieces, w_buf, sem)
    for chip in range(chips):
        started(copies[chip])
    for chip in range(chips):
        for copy in copies[chip]:
            copy.wait()
        lanes = pl.ds(pl.multiple_of(at_ref[chip] * depth, LANES), depth)
        d_hidden[:, lanes] = lax.dot_general(
            dm_ref[...], w_buf[chip], (((1,), (1,)), ((), ())), preferred_element_type=f32
        )

    @pl.loop(0, rows // 16)
    def _(block):
        at = pl.ds(pl.multiple_of(block * 16, 16), 16)
        normed, scale_inv = centred(rows_ref[at, :].astype(f32))
        grad_ref[at, :] = back_through_norm(d_hidden[at, :], normed, scale_inv).astype(bf16)


VMEM = pl.BlockSpec(memory_space=pltpu.VMEM)
SMEM = pl.BlockSpec(memory_space=pltpu.SMEM)
ANY = pl.BlockSpec(memory_space=pltpu.HBM)


def limit(mib):
    return pltpu.CompilerParams(vmem_limit_bytes=mib * 1024 * 1024)


def run_part(chips, core, from_prev, rows_in, from_next, pieces, halo):
    rows, width = rows_in.shape
    big = rows + 2 * halo
    depth = pieces[0].shape[0] * CHIP
    mixed_width = pieces[0].shape[1]
    return pl.pallas_call(
        functools.partial(part_kernel, halo),
        out_shape=(
            jax.ShapeDtypeStruct((big, width), bf16),
            jax.ShapeDtypeStruct((big, mixed_width), f32),
        ),
        in_specs=[SMEM, SMEM, VMEM, VMEM, VMEM] + [ANY] * len(pieces),
        out_specs=(VMEM, VMEM),
        scratch_shapes=[
            pltpu.VMEM((chips.shape[0], depth, mixed_width), bf16),
            pltpu.SemaphoreType.DMA((len(pieces),)),
        ],
        compiler_params=limit(44),
        cost_estimate=pl.CostEstimate(flops=2 * 10**9, bytes_accessed=8 * 10**6, transcendentals=0),
        name="forward_part",
    )(chips, core, from_prev, rows_in, from_next, *pieces)


def run_main(bounds, chips, core, corner, hidden, part, upstream, kernel, pieces, rows, edge, shares):
    big, width = hidden.shape
    wide = upstream.shape[0]
    taps = kernel.shape[0]
    depth = sum(piece.shape[0] for piece in pieces)
    return pl.pallas_call(
        functools.partial(main_kernel, rows, edge),
        out_shape=(
            jax.ShapeDtypeStruct((rows, width), bf16),
            jax.ShapeDtypeStruct((rows, 2 * width), bf16),
            jax.ShapeDtypeStruct((shares, rows, 2 * width // shares), bf16),
        ),
        in_specs=[SMEM, SMEM, SMEM, VMEM, VMEM, VMEM, VMEM, VMEM] + [ANY] * len(pieces),
        out_specs=(VMEM, VMEM, VMEM),
        scratch_shapes=[
            pltpu.VMEM((depth, 2 * width), bf16),
            pltpu.VMEM((rows, width), f32),
            pltpu.VMEM((rows, width), f32),
            pltpu.VMEM((big, width), f32),
            pltpu.VMEM((wide, width), f32),
            pltpu.VMEM((8, big, LANES), f32),
            pltpu.VMEM((taps, wide, LANES), f32),
            pltpu.SemaphoreType.DMA((len(pieces),)),
        ],
        compiler_params=limit(44),
        cost_estimate=pl.CostEstimate(flops=6 * 10**9, bytes_accessed=12 * 10**6, transcendentals=0),
        name="main",
    )(bounds, chips, core, corner, hidden, part, upstream, kernel, *pieces)


def run_frame(chips, core, rows_in, d_mixed, pieces):
    rows, width = rows_in.shape
    return pl.pallas_call(
        frame_kernel,
        out_shape=jax.ShapeDtypeStruct((rows, width), bf16),
        in_specs=[SMEM, SMEM, VMEM, VMEM] + [ANY] * len(pieces),
        out_specs=VMEM,
        scratch_shapes=[
            pltpu.VMEM((chips.shape[0], width // chips.shape[0], 2 * width), bf16),
            pltpu.VMEM((rows, width), f32),
            pltpu.SemaphoreType.DMA((len(pieces),)),
        ],
        compiler_params=limit(58),
        cost_estimate=pl.CostEstimate(flops=2 * 10**9, bytes_accessed=11 * 10**6, transcendentals=0),
        name="frame_back",
    )(chips, core, rows_in, d_mixed, *pieces)


def ring(value, axis, steps):
    count = lax.axis_size(axis)
    return lax.ppermute(value, axis, [(i, (i + steps) % count) for i in range(count)])


def other_core(value):
    return lax.ppermute(value, "c", [(0, 1), (1, 0)])


def weight_blocks(w_in):
    half = w_in.shape[0] // 2
    below, above = ring(w_in, "y", 1), ring(w_in, "y", -1)
    return below, above, [ring(below[:half], "y", 1), ring(above[half:], "y", -1)]


def exchange_edges(rows_in, cot_rows, bounds_row, device, edge):
    rows, width = rows_in.shape
    halo = 2 * edge
    sent = rows // 2 + edge
    load = bounds_row[device + 1] - bounds_row[device]
    slot = jnp.arange(cot_rows.shape[0], dtype=jnp.int32)[:, None]
    own = jnp.where(slot < load, cot_rows, jnp.zeros((), cot_rows.dtype))
    padded = jnp.concatenate([jnp.zeros((sent, width), own.dtype), own], axis=0)
    last_rows = lax.dynamic_slice_in_dim(padded, load, sent, 0)
    upwards = jnp.concatenate([rows_in[rows - halo :], last_rows], axis=0)
    downwards = jnp.concatenate([own[:sent], rows_in[:halo]], axis=0)
    return own, passed_along(upwards, SEQ, 1), passed_along(downwards, SEQ, -1)


def upstream_window(own, from_prev, from_next, bounds_row, device, rows, edge):
    came, width = from_prev.shape
    start_row = bounds_row[device]
    load = bounds_row[device + 1] - start_row
    joined = jnp.concatenate([from_prev, own, jnp.zeros((came, width), own.dtype)], axis=0)
    joined = lax.dynamic_update_slice_in_dim(joined, from_next, came + load, 0)
    first = rows * device - edge - (start_row - came)
    return lax.dynamic_slice_in_dim(joined, first, rows + 2 * edge, 0)


def owner_slots(out_rows, bounds_row, device):
    rows, width = out_rows.shape
    half = rows // 2
    from_prev = passed_along(out_rows[half:], SEQ, 1)
    from_next = passed_along(out_rows[:half], SEQ, -1)
    start_row = bounds_row[device]
    load = bounds_row[device + 1] - start_row
    joined = jnp.concatenate(
        [from_prev, out_rows, from_next, jnp.zeros((rows, width), out_rows.dtype)], axis=0
    )
    placed = lax.dynamic_slice_in_dim(joined, start_row - (rows * device - half), 2 * rows, 0)
    slot = jnp.arange(2 * rows, dtype=jnp.int32)[:, None]
    return jnp.where(slot < load, placed, jnp.zeros((), placed.dtype))


def by_receiver(hidden):
    width = hidden.shape[1]
    xs, zs, ys = lax.axis_size("x"), lax.axis_size("z"), lax.axis_size("y")
    kept = width // (xs * zs * ys)
    place = jnp.arange(width, dtype=jnp.int32)
    rest, row = place // kept, place % kept
    x, rest = rest % xs, rest // xs
    z, y = rest % zs, rest // zs
    feature = ((x * zs + z) * ys + y) * kept + row
    chosen = (place[:, None] == feature[None, :]).astype(bf16)
    return jnp.dot(hidden, chosen, preferred_element_type=f32).astype(bf16)


def hidden_blocks(hidden):
    return [ring(hidden, "x", -1), ring(hidden, "x", 2), ring(hidden, "x", 1), hidden]


def all_hidden(blocks):
    count = lax.axis_size("x")
    blocks = jnp.stack(blocks)
    others = other_core(blocks)
    core = lax.axis_index("c")
    both = jnp.stack(
        [jnp.where(core == 0, blocks, others), jnp.where(core == 0, others, blocks)], axis=1
    )
    twice = jnp.concatenate([both, both], axis=0)
    first = (count - 1 - lax.axis_index("x")) % count
    ordered = lax.dynamic_slice_in_dim(twice, first, count, 0)
    return ordered.reshape(-1, blocks.shape[-1])


def weight_gradient(hidden_all, mixed_share, frame_total, group_count):
    width = hidden_all.shape[1]
    share = mixed_share.shape[1]
    ys = lax.axis_size("y")
    y = lax.axis_index("y")
    taken = width // ys

    def product(steps):
        columns = lax.dynamic_slice_in_dim(hidden_all, taken * ((y + steps) % ys), taken, 1)
        return lax.dot_general(
            columns, mixed_share, (((0,), (0,)), ((), ())), preferred_element_type=f32
        )

    from_far = ring(product(2).astype(bf16), "y", 2).astype(f32)
    from_below = ring(product(1).astype(bf16), "y", 1).astype(f32)
    from_above = ring(product(3).astype(bf16), "y", -1).astype(f32)
    own, from_far = lax.optimization_barrier((product(0), from_far))
    summed = (own + from_far + from_below + from_above).astype(bf16)
    last = ("z", "x", "c")
    receivers = lax.axis_size(last)
    pieces = summed.reshape(receivers, taken // receivers, share)
    pieces = lax.all_to_all(pieces, last, 0, 0, tiled=True).astype(f32)
    pieces = jnp.sum(pieces.reshape(lax.axis_size("z"), -1, taken // receivers, share), axis=0)
    w_grad = jnp.swapaxes(pieces, 0, 1).reshape(taken // receivers, -1)
    return w_grad * (1.0 / math.sqrt(group_count * frame_total))


def on_device(frames, lengths, offsets, w_in, kernel, cotangent):
    rows_in = frames[0]
    rows, width = rows_in.shape
    half_width = kernel.shape[0] // 2
    edge = half_width + 1
    halo = 2 * edge
    seq_count = lax.axis_size(SEQ)
    device = lax.axis_index(SEQ)
    frame_total = seq_count * rows
    bounds_row = offsets[0]
    chip = lax.axis_index("y")
    chips = lax.axis_size("y")
    core = lax.axis_index("c").reshape(1)
    below, above, far = weight_blocks(w_in)
    own_other = other_core(w_in)
    own, from_prev, from_next = exchange_edges(
        rows_in, cotangent[0], bounds_row, device, edge
    )
    upstream = upstream_window(own, from_prev, from_next, bounds_row, device, rows, edge)
    rows_late, own_other = lax.optimization_barrier((rows_in, own_other))
    near = [w_in, own_other, below, other_core(below), above, other_core(above)]
    order = jnp.stack([chip, (chip + chips - 1) % chips, (chip + 1) % chips, (chip + 2) % chips])

    hidden_sent = by_receiver(normalize_rows(rows_late)[0].astype(bf16))
    blocks = hidden_blocks(hidden_sent)

    bounds = [rows * device - edge, jnp.int32(frame_total)]
    utt_end = jnp.int32(0)
    for utt in range(lengths.shape[1] - 1):
        utt_end = utt_end + lengths[0, utt]
        bounds.append(utt_end)
    bounds = jnp.stack(bounds).astype(jnp.int32)

    hidden, part = run_part(order[:3], core, from_prev, rows_in, from_next, near, halo)
    far, corner = lax.optimization_barrier((far, part[:8, :LANES]))
    far = far + [other_core(piece) for piece in far]
    shares = lax.axis_size(("x", "c"))
    output, d_mixed, d_shares = run_main(
        bounds, order, core, corner, hidden, part, upstream, kernel, far, rows, edge, shares
    )
    blocks, d_shares = lax.optimization_barrier((blocks, d_shares))
    hidden_all = all_hidden(blocks)
    mixed_share = lax.all_to_all(d_shares, ("x", "c"), 0, 0, tiled=True)
    mixed_share = mixed_share.reshape(shares * rows, -1)
    frame_grad = run_frame(order, core, rows_in, d_mixed, near + far)
    w_grad = weight_gradient(hidden_all, mixed_share, frame_total, chips * CHIP)
    owner_output = owner_slots(output, bounds_row, device)
    return (owner_output[None], frame_grad[None], w_grad)


def solution(mesh):
    seq_count, group_count = mesh.devices.shape
    ys, xs = group_count // CHIP, 4
    devices = mesh.devices.reshape(xs, seq_count // xs, ys, CHIP)
    groups = ("y", "c")
    return jax.shard_map(
        on_device,
        mesh=jax.sharding.Mesh(devices, ("x", "z", "y", "c")),
        in_specs=(
            P(groups, SEQ, None),
            P(groups, None),
            P(groups, None),
            P(groups, None),
            P(),
            P(groups, SEQ, None),
        ),
        out_specs=(P(groups, SEQ, None), P(groups, SEQ, None), P((*SEQ, *groups), None)),
        check_vma=False,
    )
```

```python
import functools
import math

import jax
import jax.numpy as jnp
from jax import lax
from jax.experimental import pallas as pl
from jax.experimental.pallas import tpu as pltpu
from jax.sharding import PartitionSpec as P

epsilon = 1e-05
bf16 = jnp.bfloat16
f32 = jnp.float32
LANES = 128
BLOCK = 32
SEQ = ("x", "z")
CHIP = 2
NEAR = 3


def passed_along(value, axis, steps):
    count = lax.axis_size(axis)
    initial, last = (max(0, -steps), min(count, count - steps))
    return lax.ppermute(value, axis, [(source, source + steps) for source in range(initial, last)])


def normalize_rows(values):
    values = values.astype(f32)
    center = jnp.mean(values, axis=-1, keepdims=True)
    shifted = values - center
    scale_inv = lax.rsqrt(jnp.mean(shifted * shifted, axis=-1, keepdims=True) + epsilon)
    return (shifted * scale_inv, scale_inv)


def shifted_copies(source, copies, rows):
    copies[0, :rows] = source
    for shift in range(1, 8):
        copies[shift, :rows] = pltpu.roll(source, rows - shift, 0)


def tap_sum(copies, mask_ref, ker_ref, lanes, row, mask_row, count, flip, masked):
    tap_count = ker_ref.shape[0]
    totals = [jnp.zeros((count, LANES), f32)] * 2
    for tap in range(tap_count):
        tile, shift = divmod(tap + 1, 8)
        weight = ker_ref[pl.ds(tap_count - 1 - tap if flip else tap, 1), lanes]
        term = weight * copies[shift, pl.ds(row + 8 * tile, count), :]
        if masked:
            term = term * mask_ref[tap, pl.ds(mask_row, count), :]
        totals[tap % 2] = totals[tap % 2] + term
    return totals[0] + totals[1]


def centred(values):
    inverse = 1.0 / values.shape[-1]
    center = jnp.sum(values, axis=-1, keepdims=True) * inverse
    shifted = values - center
    variance = jnp.sum(shifted * shifted, axis=-1, keepdims=True) * inverse
    scale_inv = lax.rsqrt(variance + epsilon)
    return shifted * scale_inv, scale_inv


def started(copies):
    for copy in copies:
        copy.start()
    return copies


def pair_copies(core_ref, pieces, target, sem, first):
    copies = []
    half = len(pieces) // 2
    rows = target.shape[0] // CHIP
    for index, piece in enumerate(pieces):
        count = piece.shape[0]
        core = core_ref[0] if index < half else 1 - core_ref[0]
        start = pl.multiple_of(core * rows + (index % half) * count, 16)
        copies.append(
            pltpu.make_async_copy(piece, target.at[pl.ds(start, count), :], sem.at[first + index])
        )
    return copies


def chip_copies(core_ref, pieces, w_buf, sem):
    copies = []
    first = 0
    for chip in range(w_buf.shape[0]):
        count = 2 if chip < NEAR else 4
        copies.append(pair_copies(core_ref, pieces[first : first + count], w_buf.at[chip], sem, first))
        first += count
    return copies


def part_kernel(halo, at_ref, core_ref, prev_ref, rows_ref, next_ref, *rest):
    piece_count = len(rest) - 4
    pieces = rest[:piece_count]
    hid_ref, part_ref, w_buf, sem = rest[piece_count:]
    chips = w_buf.shape[0]
    depth = w_buf.shape[1]
    copies = chip_copies(core_ref, pieces, w_buf, sem)
    for chip in range(chips):
        started(copies[chip])

    def normalize(source, first, count, target):
        @pl.loop(0, count // 16)
        def _(block):
            taken = pl.ds(pl.multiple_of(first + block * 16, 16), 16)
            put = pl.ds(pl.multiple_of(target + block * 16, 16), 16)
            hid_ref[put, :] = centred(source[taken, :].astype(f32))[0].astype(bf16)

    rows = rows_ref.shape[0]
    normalize(prev_ref, 0, halo, 0)
    normalize(rows_ref, 0, rows, halo)
    normalize(next_ref, next_ref.shape[0] - halo, halo, halo + rows)

    for chip in range(chips):
        for copy in copies[chip]:
            copy.wait()

    @pl.loop(0, part_ref.shape[1] // 256)
    def _(block):
        at = pl.ds(pl.multiple_of(block * 256, 256), 256)
        total = jnp.zeros((hid_ref.shape[0], 256), f32)
        for chip in range(chips):
            lanes = pl.ds(pl.multiple_of(at_ref[chip] * depth, LANES), depth)
            total = total + jnp.dot(
                hid_ref[:, lanes], w_buf[chip, :, at], preferred_element_type=f32
            )
        part_ref[:, at] = total


def main_kernel(rows, edge, bounds_ref, at_ref, core_ref, corner_ref, hid_ref, part_ref, up_ref, ker_ref, *rest):
    piece_count = len(rest) - 11
    pieces = rest[:piece_count]
    out_ref, dm_ref, shares_ref, w_buf, val, gate, glu, conv, copies_buf, mask_ref, sem = rest[piece_count:]
    width = hid_ref.shape[1]
    window = rows + 4 * edge
    wide = rows + 2 * edge
    tap_count = ker_ref.shape[0]
    half_width = tap_count // 2
    copies = started(pair_copies(core_ref, pieces, w_buf, sem, 0))
    depth = w_buf.shape[0]
    far = pl.ds(pl.multiple_of(at_ref[at_ref.shape[0] - 1] * depth, LANES), depth)
    base = bounds_ref[0]
    last = bounds_ref[1]
    ends = [bounds_ref[index] for index in range(2, bounds_ref.shape[0])]

    def crossed(first, count):
        found = jnp.bool_(False)
        for end in ends:
            found = found | ((end > first - half_width) & (end < first + count + half_width))
        return found

    @pl.when(crossed(base, wide))
    def _():
        @pl.loop(0, wide // 8)
        def _(block):
            row = pl.multiple_of(block * 8, 8)
            position = base + row + lax.broadcasted_iota(jnp.int32, (8, LANES), 0)
            low = jnp.zeros((8, LANES), jnp.int32)
            high = jnp.full((8, LANES), last, jnp.int32)
            for end in ends:
                low = jnp.where(position >= end, jnp.maximum(low, end), low)
                high = jnp.where(position < end, jnp.minimum(high, end), high)
            low = low - position + half_width
            high = high - position + half_width
            for tap in range(tap_count):
                mask_ref[tap, pl.ds(row, 8), :] = jnp.where((low <= tap) & (high > tap), 1.0, 0.0).astype(f32)

    for copy in copies:
        copy.wait()

    @pl.loop(0, width // 256)
    def _(block):
        at = pl.ds(pl.multiple_of(block * 256, 256), 256)
        gate_at = pl.ds(pl.multiple_of(block * 256 + width, 256), 256)
        values = part_ref[:, at] + jnp.dot(hid_ref[:, far], w_buf[:, at], preferred_element_type=f32)
        gates = jax.nn.sigmoid(
            part_ref[:, gate_at]
            + jnp.dot(hid_ref[:, far], w_buf[:, gate_at], preferred_element_type=f32)
        )
        val[:, at] = values[2 * edge : 2 * edge + rows]
        gate[:, at] = gates[2 * edge : 2 * edge + rows]
        glu[:, at] = (values * gates).astype(bf16).astype(f32)

    @pl.loop(0, width // LANES)
    def _(block):
        lanes = pl.ds(pl.multiple_of(block * LANES, LANES), LANES)
        shifted_copies(glu[:, lanes], copies_buf, window)

        @pl.loop(0, wide // BLOCK)
        def _(step):
            row = pl.multiple_of(step * BLOCK, BLOCK)
            cut = crossed(base + row, BLOCK)

            @pl.when(jnp.logical_not(cut))
            def _():
                conv[pl.ds(row, BLOCK), lanes] = tap_sum(
                    copies_buf, mask_ref, ker_ref, lanes, row, row, BLOCK, False, False
                )

            @pl.when(cut)
            def _():
                conv[pl.ds(row, BLOCK), lanes] = tap_sum(
                    copies_buf, mask_ref, ker_ref, lanes, row, row, BLOCK, False, True
                )

    @pl.loop(0, wide // 16)
    def _(block):
        at = pl.ds(pl.multiple_of(block * 16, 16), 16)
        normed, scale_inv = centred(conv[at, :])
        gates = jax.nn.sigmoid(normed)
        output = normed * gates

        @pl.when((block >= edge // 16) & (block < (edge + rows) // 16))
        def _():
            out_ref[pl.ds(pl.multiple_of(block * 16 - edge, 16), 16), :] = output.astype(bf16)

        d_normed = up_ref[at, :].astype(f32) * (gates + output * (1.0 - gates))
        conv[at, :] = back_through_norm(d_normed, normed, scale_inv)

    @pl.loop(0, width // LANES)
    def _(block):
        lanes = pl.ds(pl.multiple_of(block * LANES, LANES), LANES)
        gate_lanes = pl.ds(pl.multiple_of(block * LANES + width, LANES), LANES)
        shifted_copies(conv[:, lanes], copies_buf, wide)
        per_share = shares_ref.shape[2] // LANES
        share = lax.div(block, per_share)
        share_lanes = pl.ds(pl.multiple_of((block - share * per_share) * LANES, LANES), LANES)

        @pl.loop(0, rows // BLOCK)
        def _(step):
            row = pl.multiple_of(step * BLOCK, BLOCK)
            at = pl.ds(row, BLOCK)
            cut = crossed(base + edge + row, BLOCK)

            def finish(masked):
                d_glu = tap_sum(
                    copies_buf, mask_ref, ker_ref, lanes, row, row + edge, BLOCK, True, masked
                )
                gates = gate[at, lanes]
                d_values = d_glu * gates
                d_gates = (d_values * val[at, lanes] * (1.0 - gates)).astype(bf16)
                d_values = d_values.astype(bf16)
                dm_ref[at, lanes] = d_values
                dm_ref[at, gate_lanes] = d_gates
                shares_ref[share, at, share_lanes] = d_values
                shares_ref[share + shares_ref.shape[0] // 2, at, share_lanes] = d_gates

            @pl.when(jnp.logical_not(cut))
            def _():
                finish(False)

            @pl.when(cut)
            def _():
                finish(True)


def back_through_norm(upstream, normed, scale_inv):
    inverse = 1.0 / normed.shape[-1]
    first_mean = jnp.sum(upstream, axis=-1, keepdims=True) * inverse
    second_mean = jnp.sum(upstream * normed, axis=-1, keepdims=True) * inverse
    return scale_inv * (upstream - first_mean - normed * second_mean)


def frame_kernel(at_ref, core_ref, rows_ref, dm_ref, *rest):
    piece_count = len(rest) - 4
    pieces = rest[:piece_count]
    grad_ref, w_buf, d_hidden, sem = rest[piece_count:]
    rows, width = rows_ref.shape
    chips, depth = w_buf.shape[:2]
    copies = chip_copies(core_ref, pieces, w_buf, sem)
    for chip in range(chips):
        started(copies[chip])
    for chip in range(chips):
        for copy in copies[chip]:
            copy.wait()
        lanes = pl.ds(pl.multiple_of(at_ref[chip] * depth, LANES), depth)
        d_hidden[:, lanes] = lax.dot_general(
            dm_ref[...], w_buf[chip], (((1,), (1,)), ((), ())), preferred_element_type=f32
        )

    @pl.loop(0, rows // 16)
    def _(block):
        at = pl.ds(pl.multiple_of(block * 16, 16), 16)
        normed, scale_inv = centred(rows_ref[at, :].astype(f32))
        grad_ref[at, :] = back_through_norm(d_hidden[at, :], normed, scale_inv).astype(bf16)


VMEM = pl.BlockSpec(memory_space=pltpu.VMEM)
SMEM = pl.BlockSpec(memory_space=pltpu.SMEM)
ANY = pl.BlockSpec(memory_space=pltpu.HBM)


def limit(mib):
    return pltpu.CompilerParams(vmem_limit_bytes=mib * 1024 * 1024)


def run_part(chips, core, from_prev, rows_in, from_next, pieces, halo):
    rows, width = rows_in.shape
    big = rows + 2 * halo
    depth = pieces[0].shape[0] * CHIP
    mixed_width = pieces[0].shape[1]
    return pl.pallas_call(
        functools.partial(part_kernel, halo),
        out_shape=(
            jax.ShapeDtypeStruct((big, width), bf16),
            jax.ShapeDtypeStruct((big, mixed_width), f32),
        ),
        in_specs=[SMEM, SMEM, VMEM, VMEM, VMEM] + [ANY] * len(pieces),
        out_specs=(VMEM, VMEM),
        scratch_shapes=[
            pltpu.VMEM((chips.shape[0], depth, mixed_width), bf16),
            pltpu.SemaphoreType.DMA((len(pieces),)),
        ],
        compiler_params=limit(44),
        cost_estimate=pl.CostEstimate(flops=2 * 10**9, bytes_accessed=8 * 10**6, transcendentals=0),
        name="forward_part",
    )(chips, core, from_prev, rows_in, from_next, *pieces)


def run_main(bounds, chips, core, corner, hidden, part, upstream, kernel, pieces, rows, edge, shares):
    big, width = hidden.shape
    wide = upstream.shape[0]
    taps = kernel.shape[0]
    depth = sum(piece.shape[0] for piece in pieces)
    return pl.pallas_call(
        functools.partial(main_kernel, rows, edge),
        out_shape=(
            jax.ShapeDtypeStruct((rows, width), bf16),
            jax.ShapeDtypeStruct((rows, 2 * width), bf16),
            jax.ShapeDtypeStruct((shares, rows, 2 * width // shares), bf16),
        ),
        in_specs=[SMEM, SMEM, SMEM, VMEM, VMEM, VMEM, VMEM, VMEM] + [ANY] * len(pieces),
        out_specs=(VMEM, VMEM, VMEM),
        scratch_shapes=[
            pltpu.VMEM((depth, 2 * width), bf16),
            pltpu.VMEM((rows, width), f32),
            pltpu.VMEM((rows, width), f32),
            pltpu.VMEM((big, width), f32),
            pltpu.VMEM((wide, width), f32),
            pltpu.VMEM((8, big, LANES), f32),
            pltpu.VMEM((taps, wide, LANES), f32),
            pltpu.SemaphoreType.DMA((len(pieces),)),
        ],
        compiler_params=limit(44),
        cost_estimate=pl.CostEstimate(flops=6 * 10**9, bytes_accessed=12 * 10**6, transcendentals=0),
        name="main",
    )(bounds, chips, core, corner, hidden, part, upstream, kernel, *pieces)


def run_frame(chips, core, rows_in, d_mixed, pieces):
    rows, width = rows_in.shape
    return pl.pallas_call(
        frame_kernel,
        out_shape=jax.ShapeDtypeStruct((rows, width), bf16),
        in_specs=[SMEM, SMEM, VMEM, VMEM] + [ANY] * len(pieces),
        out_specs=VMEM,
        scratch_shapes=[
            pltpu.VMEM((chips.shape[0], width // chips.shape[0], 2 * width), bf16),
            pltpu.VMEM((rows, width), f32),
            pltpu.SemaphoreType.DMA((len(pieces),)),
        ],
        compiler_params=limit(58),
        cost_estimate=pl.CostEstimate(flops=2 * 10**9, bytes_accessed=11 * 10**6, transcendentals=0),
        name="frame_back",
    )(chips, core, rows_in, d_mixed, *pieces)


def ring(value, axis, steps):
    count = lax.axis_size(axis)
    return lax.ppermute(value, axis, [(i, (i + steps) % count) for i in range(count)])


def other_core(value):
    return lax.ppermute(value, "c", [(0, 1), (1, 0)])


def exchange_edges(rows_in, cot_rows, bounds_row, device, edge):
    rows, width = rows_in.shape
    halo = 2 * edge
    sent = rows // 2 + edge
    load = bounds_row[device + 1] - bounds_row[device]
    slot = jnp.arange(cot_rows.shape[0], dtype=jnp.int32)[:, None]
    own = jnp.where(slot < load, cot_rows, jnp.zeros((), cot_rows.dtype))
    padded = jnp.concatenate([jnp.zeros((sent, width), own.dtype), own], axis=0)
    last_rows = lax.dynamic_slice_in_dim(padded, load, sent, 0)
    upwards = jnp.concatenate([rows_in[rows - halo :], last_rows], axis=0)
    downwards = jnp.concatenate([own[:sent], rows_in[:halo]], axis=0)
    came = sent + halo
    first = rows * device - edge - (bounds_row[device] - came)
    beside = jnp.zeros((came, width), own.dtype)
    own_window = lax.dynamic_slice_in_dim(
        jnp.concatenate([beside, own, beside], axis=0), first, rows + 2 * edge, 0
    )
    return passed_along(upwards, SEQ, 1), passed_along(downwards, SEQ, -1), own_window, first, load


def upstream_window(own_window, from_prev, from_next, first, load):
    came, width = from_prev.shape
    wide = own_window.shape[0]
    most = 2 * wide
    behind = jnp.concatenate([from_prev, jnp.zeros((most - came, width), from_prev.dtype)], axis=0)
    before = 3 * came
    ahead = jnp.concatenate(
        [
            jnp.zeros((before, width), from_next.dtype),
            from_next,
            jnp.zeros((most - came, width), from_next.dtype),
        ],
        axis=0,
    )
    return (
        lax.dynamic_slice_in_dim(behind, first, wide, 0)
        + own_window
        + lax.dynamic_slice_in_dim(ahead, first - came - load + before, wide, 0)
    )


def owner_slots(out_rows, from_prev, from_next, bounds_row, device):
    rows, width = out_rows.shape
    start_row = bounds_row[device]
    load = bounds_row[device + 1] - start_row
    joined = jnp.concatenate(
        [from_prev, out_rows, from_next, jnp.zeros((rows, width), out_rows.dtype)], axis=0
    )
    placed = lax.dynamic_slice_in_dim(joined, start_row - (rows * device - rows // 2), 2 * rows, 0)
    slot = jnp.arange(2 * rows, dtype=jnp.int32)[:, None]
    return jnp.where(slot < load, placed, jnp.zeros((), placed.dtype))


def by_receiver(hidden):
    width = hidden.shape[1]
    xs, zs, ys = lax.axis_size("x"), lax.axis_size("z"), lax.axis_size("y")
    kept = width // (xs * zs * ys)
    place = jnp.arange(width, dtype=jnp.int32)
    rest, row = place // kept, place % kept
    x, rest = rest % xs, rest // xs
    z, y = rest % zs, rest // zs
    feature = ((x * zs + z) * ys + y) * kept + row
    chosen = (place[:, None] == feature[None, :]).astype(bf16)
    return jnp.dot(hidden, chosen, preferred_element_type=f32).astype(bf16)


def hidden_blocks(hidden):
    return [ring(hidden, "x", -1), ring(hidden, "x", 2), ring(hidden, "x", 1), hidden]


def all_hidden(blocks):
    count = lax.axis_size("x")
    blocks = jnp.stack(blocks)
    others = other_core(blocks)
    core = lax.axis_index("c")
    both = jnp.stack(
        [jnp.where(core == 0, blocks, others), jnp.where(core == 0, others, blocks)], axis=1
    )
    twice = jnp.concatenate([both, both], axis=0)
    first = (count - 1 - lax.axis_index("x")) % count
    ordered = lax.dynamic_slice_in_dim(twice, first, count, 0)
    return ordered.reshape(-1, blocks.shape[-1])


def weight_gradient(hidden_all, mixed_share, frame_total, group_count):
    width = hidden_all.shape[1]
    share = mixed_share.shape[1]
    ys = lax.axis_size("y")
    y = lax.axis_index("y")
    taken = width // ys

    def product(steps):
        columns = lax.dynamic_slice_in_dim(hidden_all, taken * ((y + steps) % ys), taken, 1)
        return lax.dot_general(
            columns, mixed_share, (((0,), (0,)), ((), ())), preferred_element_type=f32
        )

    from_far = ring(product(2).astype(bf16), "y", 2).astype(f32)
    from_below = ring(product(1).astype(bf16), "y", 1).astype(f32)
    from_above = ring(product(3).astype(bf16), "y", -1).astype(f32)
    own, from_far = lax.optimization_barrier((product(0), from_far))
    summed = (own + from_far + from_below + from_above).astype(bf16)
    last = ("z", "x", "c")
    receivers = lax.axis_size(last)
    pieces = summed.reshape(receivers, taken // receivers, share)
    pieces = lax.all_to_all(pieces, last, 0, 0, tiled=True).astype(f32)
    pieces = jnp.sum(pieces.reshape(lax.axis_size("z"), -1, taken // receivers, share), axis=0)
    w_grad = jnp.swapaxes(pieces, 0, 1).reshape(taken // receivers, -1)
    return w_grad * (1.0 / math.sqrt(group_count * frame_total))


def on_device(frames, lengths, offsets, w_in, kernel, cotangent):
    rows_in = frames[0]
    rows, width = rows_in.shape
    half_width = kernel.shape[0] // 2
    edge = half_width + 1
    halo = 2 * edge
    seq_count = lax.axis_size(SEQ)
    device = lax.axis_index(SEQ)
    frame_total = seq_count * rows
    bounds_row = offsets[0]
    chip = lax.axis_index("y")
    chips = lax.axis_size("y")
    core = lax.axis_index("c").reshape(1)
    own_other = other_core(w_in)
    below, above = ring(w_in, "y", 1), ring(w_in, "y", -1)
    from_prev, from_next, own_window, first, load = exchange_edges(
        rows_in, cotangent[0], bounds_row, device, edge
    )
    rows_late, own_other = lax.optimization_barrier((rows_in, own_other))
    hidden_sent = by_receiver(normalize_rows(rows_late)[0].astype(bf16))
    below, hidden_sent, from_prev, from_next = lax.optimization_barrier(
        (below, hidden_sent, from_prev, from_next)
    )
    upstream = upstream_window(own_window, from_prev, from_next, first, load)
    half = below.shape[0] // 2
    far = [ring(below[:half], "y", 1), ring(above[half:], "y", -1)]
    near = [w_in, own_other, below, other_core(below), above, other_core(above)]
    order = jnp.stack([chip, (chip + chips - 1) % chips, (chip + 1) % chips, (chip + 2) % chips])
    blocks = hidden_blocks(hidden_sent)

    bounds = [rows * device - edge, jnp.int32(frame_total)]
    utt_end = jnp.int32(0)
    for utt in range(lengths.shape[1] - 1):
        utt_end = utt_end + lengths[0, utt]
        bounds.append(utt_end)
    bounds = jnp.stack(bounds).astype(jnp.int32)

    hidden, part = run_part(order[:3], core, from_prev, rows_in, from_next, near, halo)
    far, corner, blocks[1] = lax.optimization_barrier((far, part[:8, :LANES], blocks[1]))
    far = far + [other_core(piece) for piece in far]
    shares = lax.axis_size(("x", "c"))
    output, d_mixed, d_shares = run_main(
        bounds, order, core, corner, hidden, part, upstream, kernel, far, rows, edge, shares
    )
    blocks, output = lax.optimization_barrier((blocks, output))
    hidden_all = all_hidden(blocks)
    mixed_share = lax.all_to_all(d_shares, ("x", "c"), 0, 0, tiled=True)
    out_prev = passed_along(output[rows // 2 :], SEQ, 1)
    out_next = passed_along(output[: rows // 2], SEQ, -1)
    mixed_share = mixed_share.reshape(shares * rows, -1)
    frame_grad = run_frame(order, core, rows_in, d_mixed, near + far)
    owner_output = owner_slots(output, out_prev, out_next, bounds_row, device)
    w_grad = weight_gradient(hidden_all, mixed_share, frame_total, chips * CHIP)
    return (owner_output[None], frame_grad[None], w_grad)


def solution(mesh):
    seq_count, group_count = mesh.devices.shape
    ys, xs = group_count // CHIP, 4
    devices = mesh.devices.reshape(xs, seq_count // xs, ys, CHIP)
    groups = ("y", "c")
    return jax.shard_map(
        on_device,
        mesh=jax.sharding.Mesh(devices, ("x", "z", "y", "c")),
        in_specs=(
            P(groups, SEQ, None),
            P(groups, None),
            P(groups, None),
            P(groups, None),
            P(),
            P(groups, SEQ, None),
        ),
        out_specs=(P(groups, SEQ, None), P(groups, SEQ, None), P((*SEQ, *groups), None)),
        check_vma=False,
    )
```

```python
import functools
import math

import jax
import jax.numpy as jnp
from jax import lax
from jax.experimental import pallas as pl
from jax.experimental.pallas import tpu as pltpu
from jax.sharding import PartitionSpec as P

epsilon = 1e-05
bf16 = jnp.bfloat16
f32 = jnp.float32
LANES = 128
BLOCK = 32
SEQ = ("x", "z")
CHIP = 2
NEAR = 3


def passed_along(value, axis, steps):
    count = lax.axis_size(axis)
    initial, last = (max(0, -steps), min(count, count - steps))
    return lax.ppermute(value, axis, [(source, source + steps) for source in range(initial, last)])


def normalize_rows(values):
    values = values.astype(f32)
    center = jnp.mean(values, axis=-1, keepdims=True)
    shifted = values - center
    scale_inv = lax.rsqrt(jnp.mean(shifted * shifted, axis=-1, keepdims=True) + epsilon)
    return (shifted * scale_inv, scale_inv)


def shifted_copies(source, copies, rows):
    copies[0, :rows] = source
    for shift in range(1, 8):
        copies[shift, :rows] = pltpu.roll(source, rows - shift, 0)


def tap_sum(copies, mask_ref, ker_ref, lanes, row, mask_row, count, flip, masked):
    tap_count = ker_ref.shape[0]
    totals = [jnp.zeros((count, LANES), f32)] * 2
    for tap in range(tap_count):
        tile, shift = divmod(tap + 1, 8)
        weight = ker_ref[pl.ds(tap_count - 1 - tap if flip else tap, 1), lanes]
        term = weight * copies[shift, pl.ds(row + 8 * tile, count), :]
        if masked:
            term = term * mask_ref[tap, pl.ds(mask_row, count), :]
        totals[tap % 2] = totals[tap % 2] + term
    return totals[0] + totals[1]


def centred(values):
    inverse = 1.0 / values.shape[-1]
    center = jnp.sum(values, axis=-1, keepdims=True) * inverse
    shifted = values - center
    variance = jnp.sum(shifted * shifted, axis=-1, keepdims=True) * inverse
    scale_inv = lax.rsqrt(variance + epsilon)
    return shifted * scale_inv, scale_inv


def started(copies):
    for copy in copies:
        copy.start()
    return copies


def pair_copies(core_ref, pieces, target, sem, first):
    copies = []
    half = len(pieces) // 2
    rows = target.shape[0] // CHIP
    for index, piece in enumerate(pieces):
        count = piece.shape[0]
        core = core_ref[0] if index < half else 1 - core_ref[0]
        start = pl.multiple_of(core * rows + (index % half) * count, 16)
        copies.append(
            pltpu.make_async_copy(piece, target.at[pl.ds(start, count), :], sem.at[first + index])
        )
    return copies


def chip_copies(core_ref, pieces, w_buf, sem):
    copies = []
    first = 0
    for chip in range(w_buf.shape[0]):
        count = 2 if chip < NEAR else 4
        copies.append(pair_copies(core_ref, pieces[first : first + count], w_buf.at[chip], sem, first))
        first += count
    return copies


def part_kernel(halo, at_ref, core_ref, prev_ref, rows_ref, next_ref, *rest):
    piece_count = len(rest) - 4
    pieces = rest[:piece_count]
    hid_ref, part_ref, w_buf, sem = rest[piece_count:]
    chips = w_buf.shape[0]
    depth = w_buf.shape[1]
    copies = chip_copies(core_ref, pieces, w_buf, sem)
    for chip in range(chips):
        started(copies[chip])

    def normalize(source, first, count, target):
        @pl.loop(0, count // 16)
        def _(block):
            taken = pl.ds(pl.multiple_of(first + block * 16, 16), 16)
            put = pl.ds(pl.multiple_of(target + block * 16, 16), 16)
            hid_ref[put, :] = centred(source[taken, :].astype(f32))[0].astype(bf16)

    rows = rows_ref.shape[0]
    normalize(prev_ref, 0, halo, 0)
    normalize(rows_ref, 0, rows, halo)
    normalize(next_ref, next_ref.shape[0] - halo, halo, halo + rows)

    for chip in range(chips):
        for copy in copies[chip]:
            copy.wait()

    @pl.loop(0, part_ref.shape[1] // 256)
    def _(block):
        at = pl.ds(pl.multiple_of(block * 256, 256), 256)
        total = jnp.zeros((hid_ref.shape[0], 256), f32)
        for chip in range(chips):
            lanes = pl.ds(pl.multiple_of(at_ref[chip] * depth, LANES), depth)
            total = total + jnp.dot(
                hid_ref[:, lanes], w_buf[chip, :, at], preferred_element_type=f32
            )
        part_ref[:, at] = total


def main_kernel(rows, edge, bounds_ref, at_ref, core_ref, corner_ref, hid_ref, part_ref, up_ref, ker_ref, *rest):
    piece_count = len(rest) - 11
    pieces = rest[:piece_count]
    out_ref, dm_ref, shares_ref, w_buf, val, gate, glu, conv, copies_buf, mask_ref, sem = rest[piece_count:]
    width = hid_ref.shape[1]
    window = rows + 4 * edge
    wide = rows + 2 * edge
    tap_count = ker_ref.shape[0]
    half_width = tap_count // 2
    copies = started(pair_copies(core_ref, pieces, w_buf, sem, 0))
    depth = w_buf.shape[0]
    far = pl.ds(pl.multiple_of(at_ref[at_ref.shape[0] - 1] * depth, LANES), depth)
    base = bounds_ref[0]
    last = bounds_ref[1]
    ends = [bounds_ref[index] for index in range(2, bounds_ref.shape[0])]

    def crossed(first, count):
        found = jnp.bool_(False)
        for end in ends:
            found = found | ((end > first - half_width) & (end < first + count + half_width))
        return found

    @pl.when(crossed(base, wide))
    def _():
        @pl.loop(0, wide // 8)
        def _(block):
            row = pl.multiple_of(block * 8, 8)
            position = base + row + lax.broadcasted_iota(jnp.int32, (8, LANES), 0)
            low = jnp.zeros((8, LANES), jnp.int32)
            high = jnp.full((8, LANES), last, jnp.int32)
            for end in ends:
                low = jnp.where(position >= end, jnp.maximum(low, end), low)
                high = jnp.where(position < end, jnp.minimum(high, end), high)
            low = low - position + half_width
            high = high - position + half_width
            for tap in range(tap_count):
                mask_ref[tap, pl.ds(row, 8), :] = jnp.where((low <= tap) & (high > tap), 1.0, 0.0).astype(f32)

    for copy in copies:
        copy.wait()

    @pl.loop(0, width // 256)
    def _(block):
        at = pl.ds(pl.multiple_of(block * 256, 256), 256)
        gate_at = pl.ds(pl.multiple_of(block * 256 + width, 256), 256)
        values = part_ref[:, at] + jnp.dot(hid_ref[:, far], w_buf[:, at], preferred_element_type=f32)
        gates = jax.nn.sigmoid(
            part_ref[:, gate_at]
            + jnp.dot(hid_ref[:, far], w_buf[:, gate_at], preferred_element_type=f32)
        )
        val[:, at] = values[2 * edge : 2 * edge + rows]
        gate[:, at] = gates[2 * edge : 2 * edge + rows]
        glu[:, at] = (values * gates).astype(bf16).astype(f32)

    @pl.loop(0, width // LANES)
    def _(block):
        lanes = pl.ds(pl.multiple_of(block * LANES, LANES), LANES)
        shifted_copies(glu[:, lanes], copies_buf, window)

        @pl.loop(0, wide // BLOCK)
        def _(step):
            row = pl.multiple_of(step * BLOCK, BLOCK)
            cut = crossed(base + row, BLOCK)

            @pl.when(jnp.logical_not(cut))
            def _():
                conv[pl.ds(row, BLOCK), lanes] = tap_sum(
                    copies_buf, mask_ref, ker_ref, lanes, row, row, BLOCK, False, False
                )

            @pl.when(cut)
            def _():
                conv[pl.ds(row, BLOCK), lanes] = tap_sum(
                    copies_buf, mask_ref, ker_ref, lanes, row, row, BLOCK, False, True
                )

    @pl.loop(0, wide // 16)
    def _(block):
        at = pl.ds(pl.multiple_of(block * 16, 16), 16)
        normed, scale_inv = centred(conv[at, :])
        gates = jax.nn.sigmoid(normed)
        output = normed * gates

        @pl.when((block >= edge // 16) & (block < (edge + rows) // 16))
        def _():
            out_ref[pl.ds(pl.multiple_of(block * 16 - edge, 16), 16), :] = output.astype(bf16)

        d_normed = up_ref[at, :].astype(f32) * (gates + output * (1.0 - gates))
        conv[at, :] = back_through_norm(d_normed, normed, scale_inv)

    @pl.loop(0, width // LANES)
    def _(block):
        lanes = pl.ds(pl.multiple_of(block * LANES, LANES), LANES)
        gate_lanes = pl.ds(pl.multiple_of(block * LANES + width, LANES), LANES)
        shifted_copies(conv[:, lanes], copies_buf, wide)
        per_share = shares_ref.shape[2] // LANES
        share = lax.div(block, per_share)
        share_lanes = pl.ds(pl.multiple_of((block - share * per_share) * LANES, LANES), LANES)

        @pl.loop(0, rows // BLOCK)
        def _(step):
            row = pl.multiple_of(step * BLOCK, BLOCK)
            at = pl.ds(row, BLOCK)
            cut = crossed(base + edge + row, BLOCK)

            def finish(masked):
                d_glu = tap_sum(
                    copies_buf, mask_ref, ker_ref, lanes, row, row + edge, BLOCK, True, masked
                )
                gates = gate[at, lanes]
                d_values = d_glu * gates
                d_gates = (d_values * val[at, lanes] * (1.0 - gates)).astype(bf16)
                d_values = d_values.astype(bf16)
                dm_ref[at, lanes] = d_values
                dm_ref[at, gate_lanes] = d_gates
                shares_ref[share, at, share_lanes] = d_values
                shares_ref[share + shares_ref.shape[0] // 2, at, share_lanes] = d_gates

            @pl.when(jnp.logical_not(cut))
            def _():
                finish(False)

            @pl.when(cut)
            def _():
                finish(True)


def back_through_norm(upstream, normed, scale_inv):
    inverse = 1.0 / normed.shape[-1]
    first_mean = jnp.sum(upstream, axis=-1, keepdims=True) * inverse
    second_mean = jnp.sum(upstream * normed, axis=-1, keepdims=True) * inverse
    return scale_inv * (upstream - first_mean - normed * second_mean)


def frame_kernel(at_ref, core_ref, rows_ref, dm_ref, *rest):
    piece_count = len(rest) - 4
    pieces = rest[:piece_count]
    grad_ref, w_buf, d_hidden, sem = rest[piece_count:]
    rows, width = rows_ref.shape
    chips, depth = w_buf.shape[:2]
    copies = chip_copies(core_ref, pieces, w_buf, sem)
    for chip in range(chips):
        started(copies[chip])
    for chip in range(chips):
        for copy in copies[chip]:
            copy.wait()
        lanes = pl.ds(pl.multiple_of(at_ref[chip] * depth, LANES), depth)
        d_hidden[:, lanes] = lax.dot_general(
            dm_ref[...], w_buf[chip], (((1,), (1,)), ((), ())), preferred_element_type=f32
        )

    @pl.loop(0, rows // 16)
    def _(block):
        at = pl.ds(pl.multiple_of(block * 16, 16), 16)
        normed, scale_inv = centred(rows_ref[at, :].astype(f32))
        grad_ref[at, :] = back_through_norm(d_hidden[at, :], normed, scale_inv).astype(bf16)


VMEM = pl.BlockSpec(memory_space=pltpu.VMEM)
SMEM = pl.BlockSpec(memory_space=pltpu.SMEM)
ANY = pl.BlockSpec(memory_space=pltpu.HBM)


def limit(mib):
    return pltpu.CompilerParams(vmem_limit_bytes=mib * 1024 * 1024)


def run_part(chips, core, from_prev, rows_in, from_next, pieces, halo):
    rows, width = rows_in.shape
    big = rows + 2 * halo
    depth = pieces[0].shape[0] * CHIP
    mixed_width = pieces[0].shape[1]
    return pl.pallas_call(
        functools.partial(part_kernel, halo),
        out_shape=(
            jax.ShapeDtypeStruct((big, width), bf16),
            jax.ShapeDtypeStruct((big, mixed_width), f32),
        ),
        in_specs=[SMEM, SMEM, VMEM, VMEM, VMEM] + [ANY] * len(pieces),
        out_specs=(VMEM, VMEM),
        scratch_shapes=[
            pltpu.VMEM((NEAR, depth, mixed_width), bf16),
            pltpu.SemaphoreType.DMA((len(pieces),)),
        ],
        compiler_params=limit(44),
        cost_estimate=pl.CostEstimate(flops=2 * 10**9, bytes_accessed=8 * 10**6, transcendentals=0),
        name="forward_part",
    )(chips, core, from_prev, rows_in, from_next, *pieces)


def run_main(bounds, chips, core, corner, hidden, part, upstream, kernel, pieces, rows, edge, shares):
    big, width = hidden.shape
    wide = upstream.shape[0]
    taps = kernel.shape[0]
    depth = sum(piece.shape[0] for piece in pieces)
    return pl.pallas_call(
        functools.partial(main_kernel, rows, edge),
        out_shape=(
            jax.ShapeDtypeStruct((rows, width), bf16),
            jax.ShapeDtypeStruct((rows, 2 * width), bf16),
            jax.ShapeDtypeStruct((shares, rows, 2 * width // shares), bf16),
        ),
        in_specs=[SMEM, SMEM, SMEM, VMEM, VMEM, VMEM, VMEM, VMEM] + [ANY] * len(pieces),
        out_specs=(VMEM, VMEM, VMEM),
        scratch_shapes=[
            pltpu.VMEM((depth, 2 * width), bf16),
            pltpu.VMEM((rows, width), f32),
            pltpu.VMEM((rows, width), f32),
            pltpu.VMEM((big, width), f32),
            pltpu.VMEM((wide, width), f32),
            pltpu.VMEM((8, big, LANES), f32),
            pltpu.VMEM((taps, wide, LANES), f32),
            pltpu.SemaphoreType.DMA((len(pieces),)),
        ],
        compiler_params=limit(44),
        cost_estimate=pl.CostEstimate(flops=6 * 10**9, bytes_accessed=12 * 10**6, transcendentals=0),
        name="main",
    )(bounds, chips, core, corner, hidden, part, upstream, kernel, *pieces)


def run_frame(chips, core, rows_in, d_mixed, pieces):
    rows, width = rows_in.shape
    return pl.pallas_call(
        frame_kernel,
        out_shape=jax.ShapeDtypeStruct((rows, width), bf16),
        in_specs=[SMEM, SMEM, VMEM, VMEM] + [ANY] * len(pieces),
        out_specs=VMEM,
        scratch_shapes=[
            pltpu.VMEM((chips.shape[0], width // chips.shape[0], 2 * width), bf16),
            pltpu.VMEM((rows, width), f32),
            pltpu.SemaphoreType.DMA((len(pieces),)),
        ],
        compiler_params=limit(58),
        cost_estimate=pl.CostEstimate(flops=2 * 10**9, bytes_accessed=11 * 10**6, transcendentals=0),
        name="frame_back",
    )(chips, core, rows_in, d_mixed, *pieces)


def ring(value, axis, steps):
    count = lax.axis_size(axis)
    return lax.ppermute(value, axis, [(i, (i + steps) % count) for i in range(count)])


def other_core(value):
    return lax.ppermute(value, "c", [(0, 1), (1, 0)])


def exchange_edges(rows_in, cot_rows, bounds_row, device, edge):
    rows, width = rows_in.shape
    halo = 2 * edge
    sent = rows // 2 + edge
    load = bounds_row[device + 1] - bounds_row[device]
    slot = jnp.arange(cot_rows.shape[0], dtype=jnp.int32)[:, None]
    own = jnp.where(slot < load, cot_rows, jnp.zeros((), cot_rows.dtype))
    padded = jnp.concatenate([jnp.zeros((sent, width), own.dtype), own], axis=0)
    last_rows = lax.dynamic_slice_in_dim(padded, load, sent, 0)
    upwards = jnp.concatenate([rows_in[rows - halo :], last_rows], axis=0)
    downwards = jnp.concatenate([own[:sent], rows_in[:halo]], axis=0)
    came = sent + halo
    first = rows * device - edge - (bounds_row[device] - came)
    beside = jnp.zeros((came, width), own.dtype)
    own_window = lax.dynamic_slice_in_dim(
        jnp.concatenate([beside, own, beside], axis=0), first, rows + 2 * edge, 0
    )
    return passed_along(upwards, SEQ, 1), passed_along(downwards, SEQ, -1), own_window, first, load


def upstream_window(own_window, from_prev, from_next, first, load):
    came, width = from_prev.shape
    wide = own_window.shape[0]
    most = 2 * wide
    behind = jnp.concatenate([from_prev, jnp.zeros((most - came, width), from_prev.dtype)], axis=0)
    before = 3 * came
    ahead = jnp.concatenate(
        [
            jnp.zeros((before, width), from_next.dtype),
            from_next,
            jnp.zeros((most - came, width), from_next.dtype),
        ],
        axis=0,
    )
    return (
        lax.dynamic_slice_in_dim(behind, first, wide, 0)
        + own_window
        + lax.dynamic_slice_in_dim(ahead, first - came - load + before, wide, 0)
    )


def owner_slots(out_rows, from_prev, from_next, bounds_row, device):
    rows, width = out_rows.shape
    start_row = bounds_row[device]
    load = bounds_row[device + 1] - start_row
    joined = jnp.concatenate(
        [from_prev, out_rows, from_next, jnp.zeros((rows, width), out_rows.dtype)], axis=0
    )
    placed = lax.dynamic_slice_in_dim(joined, start_row - (rows * device - rows // 2), 2 * rows, 0)
    slot = jnp.arange(2 * rows, dtype=jnp.int32)[:, None]
    return jnp.where(slot < load, placed, jnp.zeros((), placed.dtype))


def by_receiver(hidden):
    width = hidden.shape[1]
    xs, zs, ys = lax.axis_size("x"), lax.axis_size("z"), lax.axis_size("y")
    kept = width // (xs * zs * ys)
    place = jnp.arange(width, dtype=jnp.int32)
    rest, row = place // kept, place % kept
    x, rest = rest % xs, rest // xs
    z, y = rest % zs, rest // zs
    feature = ((x * zs + z) * ys + y) * kept + row
    chosen = (place[:, None] == feature[None, :]).astype(bf16)
    return jnp.dot(hidden, chosen, preferred_element_type=f32).astype(bf16)


def hidden_blocks(hidden):
    return [ring(hidden, "x", -1), ring(hidden, "x", 2), ring(hidden, "x", 1), hidden]


def all_hidden(blocks):
    count = lax.axis_size("x")
    blocks = jnp.stack(blocks)
    others = other_core(blocks)
    core = lax.axis_index("c")
    both = jnp.stack(
        [jnp.where(core == 0, blocks, others), jnp.where(core == 0, others, blocks)], axis=1
    )
    twice = jnp.concatenate([both, both], axis=0)
    first = (count - 1 - lax.axis_index("x")) % count
    ordered = lax.dynamic_slice_in_dim(twice, first, count, 0)
    return ordered.reshape(-1, blocks.shape[-1])


def weight_gradient(hidden_all, mixed_share, frame_total, group_count):
    width = hidden_all.shape[1]
    share = mixed_share.shape[1]
    ys = lax.axis_size("y")
    y = lax.axis_index("y")
    taken = width // ys

    def product(steps):
        columns = lax.dynamic_slice_in_dim(hidden_all, taken * ((y + steps) % ys), taken, 1)
        return lax.dot_general(
            columns, mixed_share, (((0,), (0,)), ((), ())), preferred_element_type=f32
        )

    from_far = ring(product(2).astype(bf16), "y", 2).astype(f32)
    from_below = ring(product(1).astype(bf16), "y", 1).astype(f32)
    from_above = ring(product(3).astype(bf16), "y", -1).astype(f32)
    own, from_far = lax.optimization_barrier((product(0), from_far))
    summed = (own + from_far + from_below + from_above).astype(bf16)
    last = ("z", "x", "c")
    receivers = lax.axis_size(last)
    pieces = summed.reshape(receivers, taken // receivers, share)
    pieces = lax.all_to_all(pieces, last, 0, 0, tiled=True).astype(f32)
    pieces = jnp.sum(pieces.reshape(lax.axis_size("z"), -1, taken // receivers, share), axis=0)
    w_grad = jnp.swapaxes(pieces, 0, 1).reshape(taken // receivers, -1)
    return w_grad * (1.0 / math.sqrt(group_count * frame_total))


def on_device(frames, lengths, offsets, w_in, kernel, cotangent):
    rows_in = frames[0]
    rows, width = rows_in.shape
    half_width = kernel.shape[0] // 2
    edge = half_width + 1
    halo = 2 * edge
    seq_count = lax.axis_size(SEQ)
    device = lax.axis_index(SEQ)
    frame_total = seq_count * rows
    bounds_row = offsets[0]
    chip = lax.axis_index("y")
    chips = lax.axis_size("y")
    core = lax.axis_index("c").reshape(1)
    own_other = other_core(w_in)
    below, above = ring(w_in, "y", 1), ring(w_in, "y", -1)
    from_prev, from_next, own_window, first, load = exchange_edges(
        rows_in, cotangent[0], bounds_row, device, edge
    )
    bounds = [rows * device - edge, jnp.int32(frame_total)]
    utt_end = jnp.int32(0)
    for utt in range(lengths.shape[1] - 1):
        utt_end = utt_end + lengths[0, utt]
        bounds.append(utt_end)
    bounds = jnp.stack(bounds).astype(jnp.int32)
    order = jnp.stack([chip, *(lax.rem(chip + steps, chips) for steps in (chips - 1, 1, 2))])
    rows_late, own_other = lax.optimization_barrier((rows_in, own_other))
    hidden_sent = by_receiver(normalize_rows(rows_late)[0].astype(bf16))
    below, hidden_sent, from_prev, from_next, first, load, bounds, order = (
        lax.optimization_barrier(
            (below, hidden_sent, from_prev, from_next, first, load, bounds, order)
        )
    )
    upstream = upstream_window(own_window, from_prev, from_next, first, load)
    half = below.shape[0] // 2
    far = [ring(below[:half], "y", 1), ring(above[half:], "y", -1)]
    near = [w_in, own_other, below, other_core(below), above, other_core(above)]
    blocks = hidden_blocks(hidden_sent)

    hidden, part = run_part(order, core, from_prev, rows_in, from_next, near, halo)
    far, corner, blocks[1], upstream = lax.optimization_barrier(
        (far, part[:8, :LANES], blocks[1], upstream)
    )
    far = far + [other_core(piece) for piece in far]
    shares = lax.axis_size(("x", "c"))
    output, d_mixed, d_shares = run_main(
        bounds, order, core, corner, hidden, part, upstream, kernel, far, rows, edge, shares
    )
    blocks, output = lax.optimization_barrier((blocks, output))
    hidden_all = all_hidden(blocks)
    mixed_share = lax.all_to_all(d_shares, ("x", "c"), 0, 0, tiled=True)
    out_prev = passed_along(output[rows // 2 :], SEQ, 1)
    out_next = passed_along(output[: rows // 2], SEQ, -1)
    mixed_share = mixed_share.reshape(shares * rows, -1)
    frame_grad = run_frame(order, core, rows_in, d_mixed, near + far)
    owner_output = owner_slots(output, out_prev, out_next, bounds_row, device)
    w_grad = weight_gradient(hidden_all, mixed_share, frame_total, chips * CHIP)
    return (owner_output[None], frame_grad[None], w_grad)


def solution(mesh):
    seq_count, group_count = mesh.devices.shape
    ys, xs = group_count // CHIP, 4
    devices = mesh.devices.reshape(xs, seq_count // xs, ys, CHIP)
    groups = ("y", "c")
    return jax.shard_map(
        on_device,
        mesh=jax.sharding.Mesh(devices, ("x", "z", "y", "c")),
        in_specs=(
            P(groups, SEQ, None),
            P(groups, None),
            P(groups, None),
            P(groups, None),
            P(),
            P(groups, SEQ, None),
        ),
        out_specs=(P(groups, SEQ, None), P(groups, SEQ, None), P((*SEQ, *groups), None)),
        check_vma=False,
    )
```

```python
import functools
import math

import jax
import jax.numpy as jnp
from jax import lax
from jax.experimental import pallas as pl
from jax.experimental.pallas import tpu as pltpu
from jax.sharding import PartitionSpec as P

epsilon = 1e-05
bf16 = jnp.bfloat16
f32 = jnp.float32
LANES = 128
BLOCK = 32
SEQ = ("x", "z")
CHIP = 2
NEAR = 3


def passed_along(value, axis, steps):
    count = lax.axis_size(axis)
    initial, last = (max(0, -steps), min(count, count - steps))
    return lax.ppermute(value, axis, [(source, source + steps) for source in range(initial, last)])


def normalize_rows(values):
    values = values.astype(f32)
    center = jnp.mean(values, axis=-1, keepdims=True)
    shifted = values - center
    scale_inv = lax.rsqrt(jnp.mean(shifted * shifted, axis=-1, keepdims=True) + epsilon)
    return (shifted * scale_inv, scale_inv)


def shifted_copies(source, copies, rows):
    copies[0, :rows] = source
    for shift in range(1, 8):
        copies[shift, :rows] = pltpu.roll(source, rows - shift, 0)


def tap_sum(copies, mask_ref, ker_ref, lanes, row, mask_row, count, flip, masked):
    tap_count = ker_ref.shape[0]
    totals = [jnp.zeros((count, LANES), f32)] * 2
    for tap in range(tap_count):
        tile, shift = divmod(tap + 1, 8)
        weight = ker_ref[pl.ds(tap_count - 1 - tap if flip else tap, 1), lanes]
        term = weight * copies[shift, pl.ds(row + 8 * tile, count), :]
        if masked:
            term = term * mask_ref[tap, pl.ds(mask_row, count), :]
        totals[tap % 2] = totals[tap % 2] + term
    return totals[0] + totals[1]


def centred(values):
    inverse = 1.0 / values.shape[-1]
    center = jnp.sum(values, axis=-1, keepdims=True) * inverse
    shifted = values - center
    variance = jnp.sum(shifted * shifted, axis=-1, keepdims=True) * inverse
    scale_inv = lax.rsqrt(variance + epsilon)
    return shifted * scale_inv, scale_inv


def started(copies):
    for copy in copies:
        copy.start()
    return copies


def pair_copies(core_ref, pieces, target, sem, first):
    copies = []
    half = len(pieces) // 2
    rows = target.shape[0] // CHIP
    for index, piece in enumerate(pieces):
        count = piece.shape[0]
        core = core_ref[0] if index < half else 1 - core_ref[0]
        start = pl.multiple_of(core * rows + (index % half) * count, 16)
        copies.append(
            pltpu.make_async_copy(piece, target.at[pl.ds(start, count), :], sem.at[first + index])
        )
    return copies


def chip_copies(core_ref, pieces, w_buf, sem):
    copies = []
    first = 0
    for chip in range(w_buf.shape[0]):
        count = 2 if chip < NEAR else 4
        copies.append(pair_copies(core_ref, pieces[first : first + count], w_buf.at[chip], sem, first))
        first += count
    return copies


def part_kernel(halo, at_ref, core_ref, prev_ref, rows_ref, next_ref, *rest):
    piece_count = len(rest) - 4
    pieces = rest[:piece_count]
    hid_ref, part_ref, w_buf, sem = rest[piece_count:]
    chips = w_buf.shape[0]
    depth = w_buf.shape[1]
    copies = chip_copies(core_ref, pieces, w_buf, sem)
    for chip in range(chips):
        started(copies[chip])

    def normalize(source, first, count, target):
        @pl.loop(0, count // 16)
        def _(block):
            taken = pl.ds(pl.multiple_of(first + block * 16, 16), 16)
            put = pl.ds(pl.multiple_of(target + block * 16, 16), 16)
            hid_ref[put, :] = centred(source[taken, :].astype(f32))[0].astype(bf16)

    rows = rows_ref.shape[0]
    normalize(prev_ref, 0, halo, 0)
    normalize(rows_ref, 0, rows, halo)
    normalize(next_ref, next_ref.shape[0] - halo, halo, halo + rows)

    for chip in range(chips):
        for copy in copies[chip]:
            copy.wait()

    @pl.loop(0, part_ref.shape[1] // 256)
    def _(block):
        at = pl.ds(pl.multiple_of(block * 256, 256), 256)
        total = jnp.zeros((hid_ref.shape[0], 256), f32)
        for chip in range(chips):
            lanes = pl.ds(pl.multiple_of(at_ref[chip] * depth, LANES), depth)
            total = total + jnp.dot(
                hid_ref[:, lanes], w_buf[chip, :, at], preferred_element_type=f32
            )
        part_ref[:, at] = total


def main_kernel(rows, edge, bounds_ref, at_ref, core_ref, corner_ref, hid_ref, part_ref, up_ref, ker_ref, *rest):
    piece_count = len(rest) - 11
    pieces = rest[:piece_count]
    out_ref, dm_ref, shares_ref, w_buf, val, gate, glu, conv, copies_buf, mask_ref, sem = rest[piece_count:]
    width = hid_ref.shape[1]
    window = rows + 4 * edge
    wide = rows + 2 * edge
    tap_count = ker_ref.shape[0]
    half_width = tap_count // 2
    copies = started(pair_copies(core_ref, pieces, w_buf, sem, 0))
    depth = w_buf.shape[0]
    far = pl.ds(pl.multiple_of(at_ref[at_ref.shape[0] - 1] * depth, LANES), depth)
    base = bounds_ref[0]
    last = bounds_ref[1]
    ends = [bounds_ref[index] for index in range(2, bounds_ref.shape[0])]

    def crossed(first, count):
        found = jnp.bool_(False)
        for end in ends:
            found = found | ((end > first - half_width) & (end < first + count + half_width))
        return found

    @pl.when(crossed(base, wide))
    def _():
        @pl.loop(0, wide // 8)
        def _(block):
            row = pl.multiple_of(block * 8, 8)
            position = base + row + lax.broadcasted_iota(jnp.int32, (8, LANES), 0)
            low = jnp.zeros((8, LANES), jnp.int32)
            high = jnp.full((8, LANES), last, jnp.int32)
            for end in ends:
                low = jnp.where(position >= end, jnp.maximum(low, end), low)
                high = jnp.where(position < end, jnp.minimum(high, end), high)
            low = low - position + half_width
            high = high - position + half_width
            for tap in range(tap_count):
                mask_ref[tap, pl.ds(row, 8), :] = jnp.where((low <= tap) & (high > tap), 1.0, 0.0).astype(f32)

    for copy in copies:
        copy.wait()

    @pl.loop(0, width // 256)
    def _(block):
        at = pl.ds(pl.multiple_of(block * 256, 256), 256)
        gate_at = pl.ds(pl.multiple_of(block * 256 + width, 256), 256)
        values = part_ref[:, at] + jnp.dot(hid_ref[:, far], w_buf[:, at], preferred_element_type=f32)
        gates = jax.nn.sigmoid(
            part_ref[:, gate_at]
            + jnp.dot(hid_ref[:, far], w_buf[:, gate_at], preferred_element_type=f32)
        )
        val[:, at] = values[2 * edge : 2 * edge + rows]
        gate[:, at] = gates[2 * edge : 2 * edge + rows]
        glu[:, at] = (values * gates).astype(bf16).astype(f32)

    @pl.loop(0, width // LANES)
    def _(block):
        lanes = pl.ds(pl.multiple_of(block * LANES, LANES), LANES)
        shifted_copies(glu[:, lanes], copies_buf, window)

        @pl.loop(0, wide // BLOCK)
        def _(step):
            row = pl.multiple_of(step * BLOCK, BLOCK)
            cut = crossed(base + row, BLOCK)

            @pl.when(jnp.logical_not(cut))
            def _():
                conv[pl.ds(row, BLOCK), lanes] = tap_sum(
                    copies_buf, mask_ref, ker_ref, lanes, row, row, BLOCK, False, False
                )

            @pl.when(cut)
            def _():
                conv[pl.ds(row, BLOCK), lanes] = tap_sum(
                    copies_buf, mask_ref, ker_ref, lanes, row, row, BLOCK, False, True
                )

    @pl.loop(0, wide // 16)
    def _(block):
        at = pl.ds(pl.multiple_of(block * 16, 16), 16)
        normed, scale_inv = centred(conv[at, :])
        gates = jax.nn.sigmoid(normed)
        output = normed * gates

        @pl.when((block >= edge // 16) & (block < (edge + rows) // 16))
        def _():
            out_ref[pl.ds(pl.multiple_of(block * 16 - edge, 16), 16), :] = output.astype(bf16)

        d_normed = up_ref[at, :].astype(f32) * (gates + output * (1.0 - gates))
        conv[at, :] = back_through_norm(d_normed, normed, scale_inv)

    @pl.loop(0, width // LANES)
    def _(block):
        lanes = pl.ds(pl.multiple_of(block * LANES, LANES), LANES)
        gate_lanes = pl.ds(pl.multiple_of(block * LANES + width, LANES), LANES)
        shifted_copies(conv[:, lanes], copies_buf, wide)
        per_share = shares_ref.shape[2] // LANES
        share = lax.div(block, per_share)
        share_lanes = pl.ds(pl.multiple_of((block - share * per_share) * LANES, LANES), LANES)

        @pl.loop(0, rows // BLOCK)
        def _(step):
            row = pl.multiple_of(step * BLOCK, BLOCK)
            at = pl.ds(row, BLOCK)
            cut = crossed(base + edge + row, BLOCK)

            def finish(masked):
                d_glu = tap_sum(
                    copies_buf, mask_ref, ker_ref, lanes, row, row + edge, BLOCK, True, masked
                )
                gates = gate[at, lanes]
                d_values = d_glu * gates
                d_gates = (d_values * val[at, lanes] * (1.0 - gates)).astype(bf16)
                d_values = d_values.astype(bf16)
                dm_ref[at, lanes] = d_values
                dm_ref[at, gate_lanes] = d_gates
                shares_ref[share, at, share_lanes] = d_values
                shares_ref[share + shares_ref.shape[0] // 2, at, share_lanes] = d_gates

            @pl.when(jnp.logical_not(cut))
            def _():
                finish(False)

            @pl.when(cut)
            def _():
                finish(True)


def back_through_norm(upstream, normed, scale_inv):
    inverse = 1.0 / normed.shape[-1]
    first_mean = jnp.sum(upstream, axis=-1, keepdims=True) * inverse
    second_mean = jnp.sum(upstream * normed, axis=-1, keepdims=True) * inverse
    return scale_inv * (upstream - first_mean - normed * second_mean)


def frame_kernel(at_ref, core_ref, rows_ref, dm_ref, *rest):
    piece_count = len(rest) - 4
    pieces = rest[:piece_count]
    grad_ref, w_buf, d_hidden, sem = rest[piece_count:]
    rows, width = rows_ref.shape
    chips, depth = w_buf.shape[:2]
    copies = chip_copies(core_ref, pieces, w_buf, sem)
    for chip in range(chips):
        started(copies[chip])
    for chip in range(chips):
        for copy in copies[chip]:
            copy.wait()
        lanes = pl.ds(pl.multiple_of(at_ref[chip] * depth, LANES), depth)
        d_hidden[:, lanes] = lax.dot_general(
            dm_ref[...], w_buf[chip], (((1,), (1,)), ((), ())), preferred_element_type=f32
        )

    @pl.loop(0, rows // 16)
    def _(block):
        at = pl.ds(pl.multiple_of(block * 16, 16), 16)
        normed, scale_inv = centred(rows_ref[at, :].astype(f32))
        grad_ref[at, :] = back_through_norm(d_hidden[at, :], normed, scale_inv).astype(bf16)


VMEM = pl.BlockSpec(memory_space=pltpu.VMEM)
SMEM = pl.BlockSpec(memory_space=pltpu.SMEM)
ANY = pl.BlockSpec(memory_space=pltpu.HBM)


def limit(mib):
    return pltpu.CompilerParams(vmem_limit_bytes=mib * 1024 * 1024)


def run_part(chips, core, from_prev, rows_in, from_next, pieces, halo):
    rows, width = rows_in.shape
    big = rows + 2 * halo
    depth = pieces[0].shape[0] * CHIP
    mixed_width = pieces[0].shape[1]
    return pl.pallas_call(
        functools.partial(part_kernel, halo),
        out_shape=(
            jax.ShapeDtypeStruct((big, width), bf16),
            jax.ShapeDtypeStruct((big, mixed_width), f32),
        ),
        in_specs=[SMEM, SMEM, VMEM, VMEM, VMEM] + [ANY] * len(pieces),
        out_specs=(VMEM, VMEM),
        scratch_shapes=[
            pltpu.VMEM((NEAR, depth, mixed_width), bf16),
            pltpu.SemaphoreType.DMA((len(pieces),)),
        ],
        compiler_params=limit(32),
        cost_estimate=pl.CostEstimate(flops=2 * 10**9, bytes_accessed=8 * 10**6, transcendentals=0),
        name="forward_part",
    )(chips, core, from_prev, rows_in, from_next, *pieces)


def run_main(bounds, chips, core, corner, hidden, part, upstream, kernel, pieces, rows, edge, shares):
    big, width = hidden.shape
    wide = upstream.shape[0]
    taps = kernel.shape[0]
    depth = sum(piece.shape[0] for piece in pieces)
    return pl.pallas_call(
        functools.partial(main_kernel, rows, edge),
        out_shape=(
            jax.ShapeDtypeStruct((rows, width), bf16),
            jax.ShapeDtypeStruct((rows, 2 * width), bf16),
            jax.ShapeDtypeStruct((shares, rows, 2 * width // shares), bf16),
        ),
        in_specs=[SMEM, SMEM, SMEM, VMEM, VMEM, VMEM, VMEM, VMEM] + [ANY] * len(pieces),
        out_specs=(VMEM, VMEM, VMEM),
        scratch_shapes=[
            pltpu.VMEM((depth, 2 * width), bf16),
            pltpu.VMEM((rows, width), f32),
            pltpu.VMEM((rows, width), f32),
            pltpu.VMEM((big, width), f32),
            pltpu.VMEM((wide, width), f32),
            pltpu.VMEM((8, big, LANES), f32),
            pltpu.VMEM((taps, wide, LANES), f32),
            pltpu.SemaphoreType.DMA((len(pieces),)),
        ],
        compiler_params=limit(32),
        cost_estimate=pl.CostEstimate(flops=6 * 10**9, bytes_accessed=12 * 10**6, transcendentals=0),
        name="main",
    )(bounds, chips, core, corner, hidden, part, upstream, kernel, *pieces)


def run_frame(chips, core, rows_in, d_mixed, pieces):
    rows, width = rows_in.shape
    return pl.pallas_call(
        frame_kernel,
        out_shape=jax.ShapeDtypeStruct((rows, width), bf16),
        in_specs=[SMEM, SMEM, VMEM, VMEM] + [ANY] * len(pieces),
        out_specs=VMEM,
        scratch_shapes=[
            pltpu.VMEM((chips.shape[0], width // chips.shape[0], 2 * width), bf16),
            pltpu.VMEM((rows, width), f32),
            pltpu.SemaphoreType.DMA((len(pieces),)),
        ],
        compiler_params=limit(58),
        cost_estimate=pl.CostEstimate(flops=2 * 10**9, bytes_accessed=11 * 10**6, transcendentals=0),
        name="frame_back",
    )(chips, core, rows_in, d_mixed, *pieces)


def ring(value, axis, steps):
    count = lax.axis_size(axis)
    return lax.ppermute(value, axis, [(i, (i + steps) % count) for i in range(count)])


def other_core(value):
    return lax.ppermute(value, "c", [(0, 1), (1, 0)])


def exchange_edges(rows_in, cot_rows, bounds_row, device, edge):
    rows, width = rows_in.shape
    halo = 2 * edge
    sent = rows // 2 + edge
    load = bounds_row[device + 1] - bounds_row[device]
    slot = jnp.arange(cot_rows.shape[0], dtype=jnp.int32)[:, None]
    own = jnp.where(slot < load, cot_rows, jnp.zeros((), cot_rows.dtype))
    padded = jnp.concatenate([jnp.zeros((sent, width), own.dtype), own], axis=0)
    last_rows = lax.dynamic_slice_in_dim(padded, load, sent, 0)
    upwards = jnp.concatenate([rows_in[rows - halo :], last_rows], axis=0)
    downwards = jnp.concatenate([own[:sent], rows_in[:halo]], axis=0)
    came = sent + halo
    first = rows * device - edge - (bounds_row[device] - came)
    beside = jnp.zeros((came, width), own.dtype)
    own_window = lax.dynamic_slice_in_dim(
        jnp.concatenate([beside, own, beside], axis=0), first, rows + 2 * edge, 0
    )
    return passed_along(upwards, SEQ, 1), passed_along(downwards, SEQ, -1), own_window, first, load


def upstream_window(own_window, from_prev, from_next, first, load):
    came, width = from_prev.shape
    wide = own_window.shape[0]
    most = 2 * wide
    behind = jnp.concatenate([from_prev, jnp.zeros((most - came, width), from_prev.dtype)], axis=0)
    before = 3 * came
    ahead = jnp.concatenate(
        [
            jnp.zeros((before, width), from_next.dtype),
            from_next,
            jnp.zeros((most - came, width), from_next.dtype),
        ],
        axis=0,
    )
    return (
        lax.dynamic_slice_in_dim(behind, first, wide, 0)
        + own_window
        + lax.dynamic_slice_in_dim(ahead, first - came - load + before, wide, 0)
    )


def owner_slots(out_rows, from_prev, from_next, bounds_row, device):
    rows, width = out_rows.shape
    start_row = bounds_row[device]
    load = bounds_row[device + 1] - start_row
    joined = jnp.concatenate(
        [from_prev, out_rows, from_next, jnp.zeros((rows, width), out_rows.dtype)], axis=0
    )
    placed = lax.dynamic_slice_in_dim(joined, start_row - (rows * device - rows // 2), 2 * rows, 0)
    slot = jnp.arange(2 * rows, dtype=jnp.int32)[:, None]
    return jnp.where(slot < load, placed, jnp.zeros((), placed.dtype))


def by_receiver(hidden):
    width = hidden.shape[1]
    xs, zs, ys = lax.axis_size("x"), lax.axis_size("z"), lax.axis_size("y")
    kept = width // (xs * zs * ys)
    place = jnp.arange(width, dtype=jnp.int32)
    rest, row = place // kept, place % kept
    x, rest = rest % xs, rest // xs
    z, y = rest % zs, rest // zs
    feature = ((x * zs + z) * ys + y) * kept + row
    chosen = (place[:, None] == feature[None, :]).astype(bf16)
    return jnp.dot(hidden, chosen, preferred_element_type=f32).astype(bf16)


def hidden_blocks(hidden):
    return [ring(hidden, "x", -1), ring(hidden, "x", 2), ring(hidden, "x", 1), hidden]


def all_hidden(blocks):
    count = lax.axis_size("x")
    blocks = jnp.stack(blocks)
    others = other_core(blocks)
    core = lax.axis_index("c")
    both = jnp.stack(
        [jnp.where(core == 0, blocks, others), jnp.where(core == 0, others, blocks)], axis=1
    )
    twice = jnp.concatenate([both, both], axis=0)
    first = (count - 1 - lax.axis_index("x")) % count
    ordered = lax.dynamic_slice_in_dim(twice, first, count, 0)
    return ordered.reshape(-1, blocks.shape[-1])


def weight_gradient(hidden_all, mixed_share, frame_total, group_count):
    width = hidden_all.shape[1]
    share = mixed_share.shape[1]
    ys = lax.axis_size("y")
    y = lax.axis_index("y")
    taken = width // ys

    def product(steps):
        columns = lax.dynamic_slice_in_dim(hidden_all, taken * ((y + steps) % ys), taken, 1)
        return lax.dot_general(
            columns, mixed_share, (((0,), (0,)), ((), ())), preferred_element_type=f32
        )

    from_far = ring(product(2).astype(bf16), "y", 2).astype(f32)
    from_below = ring(product(1).astype(bf16), "y", 1).astype(f32)
    from_above = ring(product(3).astype(bf16), "y", -1).astype(f32)
    own, from_far = lax.optimization_barrier((product(0), from_far))
    summed = (own + from_far + from_below + from_above).astype(bf16)
    last = ("z", "x", "c")
    receivers = lax.axis_size(last)
    pieces = summed.reshape(receivers, taken // receivers, share)
    pieces = lax.all_to_all(pieces, last, 0, 0, tiled=True).astype(f32)
    pieces = jnp.sum(pieces.reshape(lax.axis_size("z"), -1, taken // receivers, share), axis=0)
    w_grad = jnp.swapaxes(pieces, 0, 1).reshape(taken // receivers, -1)
    return w_grad * (1.0 / math.sqrt(group_count * frame_total))


def on_device(frames, lengths, offsets, w_in, kernel, cotangent):
    rows_in = frames[0]
    rows, width = rows_in.shape
    half_width = kernel.shape[0] // 2
    edge = half_width + 1
    halo = 2 * edge
    seq_count = lax.axis_size(SEQ)
    device = lax.axis_index(SEQ)
    frame_total = seq_count * rows
    bounds_row = offsets[0]
    chip = lax.axis_index("y")
    chips = lax.axis_size("y")
    core = lax.axis_index("c").reshape(1)
    own_other = other_core(w_in)
    below, above = ring(w_in, "y", 1), ring(w_in, "y", -1)
    from_prev, from_next, own_window, first, load = exchange_edges(
        rows_in, cotangent[0], bounds_row, device, edge
    )
    bounds = [rows * device - edge, jnp.int32(frame_total)]
    utt_end = jnp.int32(0)
    for utt in range(lengths.shape[1] - 1):
        utt_end = utt_end + lengths[0, utt]
        bounds.append(utt_end)
    bounds = jnp.stack(bounds).astype(jnp.int32)
    order = jnp.stack([chip, *(lax.rem(chip + steps, chips) for steps in (chips - 1, 1, 2))])
    rows_late, own_other = lax.optimization_barrier((rows_in, own_other))
    hidden_sent = by_receiver(normalize_rows(rows_late)[0].astype(bf16))
    below, hidden_sent, from_prev, from_next, first, load, bounds, order = (
        lax.optimization_barrier(
            (below, hidden_sent, from_prev, from_next, first, load, bounds, order)
        )
    )
    upstream = upstream_window(own_window, from_prev, from_next, first, load)
    half = below.shape[0] // 2
    far = [ring(below[:half], "y", 1), ring(above[half:], "y", -1)]
    near = [w_in, own_other, below, other_core(below), above, other_core(above)]
    blocks = hidden_blocks(hidden_sent)

    hidden, part = run_part(order, core, from_prev, rows_in, from_next, near, halo)
    far, corner, blocks[1], upstream = lax.optimization_barrier(
        (far, part[:8, :LANES], blocks[1], upstream)
    )
    far = far + [other_core(piece) for piece in far]
    shares = lax.axis_size(("x", "c"))
    output, d_mixed, d_shares = run_main(
        bounds, order, core, corner, hidden, part, upstream, kernel, far, rows, edge, shares
    )
    blocks, output = lax.optimization_barrier((blocks, output))
    hidden_all = all_hidden(blocks)
    mixed_share = lax.all_to_all(d_shares, ("x", "c"), 0, 0, tiled=True)
    out_prev = passed_along(output[rows // 2 :], SEQ, 1)
    out_next = passed_along(output[: rows // 2], SEQ, -1)
    mixed_share = mixed_share.reshape(shares * rows, -1)
    frame_grad = run_frame(order, core, rows_in, d_mixed, near + far)
    owner_output = owner_slots(output, out_prev, out_next, bounds_row, device)
    w_grad = weight_gradient(hidden_all, mixed_share, frame_total, chips * CHIP)
    return (owner_output[None], frame_grad[None], w_grad)


def solution(mesh):
    seq_count, group_count = mesh.devices.shape
    ys, xs = group_count // CHIP, 4
    devices = mesh.devices.reshape(xs, seq_count // xs, ys, CHIP)
    groups = ("y", "c")
    return jax.shard_map(
        on_device,
        mesh=jax.sharding.Mesh(devices, ("x", "z", "y", "c")),
        in_specs=(
            P(groups, SEQ, None),
            P(groups, None),
            P(groups, None),
            P(groups, None),
            P(),
            P(groups, SEQ, None),
        ),
        out_specs=(P(groups, SEQ, None), P(groups, SEQ, None), P((*SEQ, *groups), None)),
        check_vma=False,
    )
```
